256 devices in a mesh: img: 64 (over x_lo, y, z), tok: 4 (over x_hi, core).
Axes of the slice: x: 4 (x_hi: 2, x_lo: 2; x = x_hi * 2 + x_lo), y: 4, z: 8, core: 2. Of those that a mesh axis runs over, the one named last changes fastest.
Arguments:
- residuals: float32 [64, 32, 265], P('img', 'tok'), may hold values from -6 to 6
- stream: bfloat16 [64, 544, 1024], P('img', 'tok'), may hold values from -6 to 6
- token_slot: int32 [64, 521], P('img'), may hold values from 0 to 543, as said below
- level_embed: bfloat16 [7, 1024], replicated, may hold values from -3 to 3
- embed_weight: bfloat16 [32, 1024], replicated, may hold values from -1 to 1
- norm_gain: float32 [1024], replicated, may hold values from 0.1 to 1.9
- qkv_weight: bfloat16 [1024, 3072], replicated, may hold values from -2.5 to 2.5
- out_weight: bfloat16 [1024, 1024], replicated, may hold values from -0.1875 to 0.1875
- out_grad: bfloat16 [64, 544, 1024], P('img', 'tok'), may hold values from -0.625 to 0.625
Outputs:
- block_out: bfloat16 [64, 544, 1024], P('img', 'tok')
- qkv_weight_grad: float32 [1024, 3, 1024], P('img', None, 'tok')
- out_weight_grad: float32 [1024, 1024], P('img', 'tok')
The draws below stay inside these ranges and needn't reach their ends.
Inputs may be any that keep to these rules, and one draw needn't show every extreme that they name: `token_slot`: within an image the slots are distinct; the token in slot t is held by tok index t // 136; the last slot is always taken.
All inputs are finite; a program needn't handle non-finite values.
Results may differ from the reference program's by a relative error of at most 0.024.
Values may be sent and summed in bfloat16 or wider, within the bound.
A program may use at most 128 MiB of HBM per device.

```python
import jax
import jax.numpy as jnp
import numpy as np
from jax import lax

D = 1024
HEADS = 8
HEAD_DIM = 128
CH = 32
NSCALE = 7
TOK_IMG = 521
TOK_IN = 265
IMAGES = 64
SLOT = 136
N_TOK = 4


def draw_token_slot(key, part):
    key = jax.random.fold_in(key, 7)
    total_slots = N_TOK * SLOT

    def one_image(image_key):
        spare_slots = jax.random.permutation(image_key, total_slots - 1)[:TOK_IMG - 1].astype(jnp.int32)
        chosen = jnp.concatenate([spare_slots, jnp.full((1,), total_slots - 1, jnp.int32)])
        shuffle = jax.random.permutation(jax.random.fold_in(image_key, 1), TOK_IMG)
        return chosen[shuffle].astype(jnp.int32)
    return jax.vmap(one_image)(jax.random.split(key, IMAGES))


def draw_qkv_weight(key, part):
    key = jax.random.fold_in(key, 11)
    width_attn = HEADS * HEAD_DIM
    matrix = jnp.clip(jax.random.normal(key, (D, 3 * width_attn), jnp.float32), -4.0, 4.0) * D ** (-0.5)
    return matrix.astype(jnp.bfloat16)


def steps_of(stream_key, shape, shards, smallest, high):
    def one(axis_at, blocks):
        heights = jax.random.uniform(jax.random.fold_in(jax.random.fold_in(stream_key, 6), axis_at), (blocks,), jnp.float32, smallest / len(shards), high / len(shards))
        return jnp.repeat(jnp.exp(heights), shape[axis_at] // blocks).reshape((-1,) + (1,) * (len(shape) - axis_at - 1))

    gain = one(*shards[0])
    for cut in shards[1:]:
        gain = gain * one(*cut)
    return gain


def centred(own_key, dims, width, reach, cuts=(), kind=jnp.bfloat16):
    gain = steps_of(own_key, dims, cuts, -0.22, 0.18) if cuts else 1.0
    values = jax.random.normal(own_key, dims, jnp.float32) * width * gain
    return jnp.minimum(jnp.maximum(values, -reach), reach).astype(kind)


def setup_inputs(seed: int = 0) -> dict:
    seeds = jax.random.split(jax.random.key(seed), 10)
    return {
        "residuals": centred(seeds[0], (IMAGES, CH, TOK_IN), 1.0, 6.0, ((0, 64), (1, 4)), jnp.float32),
        "stream": centred(seeds[1], (IMAGES, N_TOK * SLOT, D), 1.0, 6.0, ((0, 64), (1, 4))),
        "token_slot": draw_token_slot(jax.random.fold_in(seeds[9], 71), 0),
        "level_embed": centred(seeds[3], (NSCALE, D), 0.5, 3.0),
        "embed_weight": centred(seeds[4], (CH, D), CH ** -0.5, 1.0),
        "norm_gain": jnp.clip(1.0 + 0.18 * jax.random.normal(seeds[5], (D,), jnp.float32), 0.1, 1.9),
        "qkv_weight": draw_qkv_weight(jax.random.fold_in(seeds[9], 71), 0),
        "out_weight": centred(seeds[7], (D, HEADS * HEAD_DIM), (HEADS * HEAD_DIM) ** -0.5, 0.1875),
        "out_grad": centred(seeds[8], (IMAGES, N_TOK * SLOT, D), (8 * (IMAGES * TOK_IMG) ** -0.5), 0.625, ((0, 64), (1, 4))),
    }


scale_sides = (1, 2, 4, 6, 8, 12, 16, 20)

def line_matrix(source, target):
    places = np.arange(target)
    numerator = (2 * places + 1) * source - target
    low_index = numerator // (2 * target)
    fraction = (numerator - low_index * 2 * target) / (2.0 * target)
    fraction = np.where(numerator < 0, 0.0, fraction)
    low_index = np.maximum(low_index, 0)
    fraction = np.where(low_index >= source - 1, 0.0, fraction)
    low_index = np.minimum(low_index, source - 1)
    high_index = np.minimum(low_index + 1, source - 1)
    columns = np.arange(source)
    return (columns[None, :] == low_index[:, None]) * (1.0 - fraction[:, None]) + (columns[None, :] == high_index[:, None]) * fraction[:, None]

def token_scales():
    grid_sides = scale_sides[:NSCALE]
    return np.repeat(np.arange(NSCALE), [grid_side * grid_side for grid_side in grid_sides]).astype(np.int32)

def teacher_maps(residuals):
    grid_sides = scale_sides[:NSCALE]
    finest = grid_sides[-1]
    leading = residuals.shape[:-1]
    canvas = jnp.zeros(leading + (finest, finest), residuals.dtype)
    pieces = [jnp.zeros(leading + (1,), residuals.dtype)]
    offset = 0
    for scale_level in range(NSCALE - 1):
        grid_side = grid_sides[scale_level]
        block_map = residuals[..., offset:offset + grid_side * grid_side].reshape(leading + (grid_side, grid_side))
        offset = offset + grid_side * grid_side
        upward = jnp.asarray(line_matrix(grid_side, finest), residuals.dtype)
        canvas = canvas + jnp.einsum('ia,...ab,jb->...ij', upward, block_map, upward, precision=lax.Precision.HIGHEST)
        next_side = grid_sides[scale_level + 1]
        downward = jnp.asarray(line_matrix(finest, next_side), residuals.dtype)
        coarse = jnp.einsum('ia,...ab,jb->...ij', downward, canvas, downward, precision=lax.Precision.HIGHEST)
        pieces.append(coarse.reshape(leading + (next_side * next_side,)))
    return jnp.concatenate(pieces, axis=-1)

def image_terms(residual, stream_img, slots, cotangent, level_embed, embed_weight, norm_gain, qkv_weight, out_weight):
    width_attn = HEADS * HEAD_DIM
    factor = HEAD_DIM ** (-0.5)
    scale_ids = jnp.asarray(token_scales())
    teacher = teacher_maps(residual).astype(jnp.bfloat16)
    stream_rows = stream_img[slots].astype(jnp.float32)
    block_in = (jnp.dot(teacher.T, embed_weight, preferred_element_type=jnp.float32) + level_embed[scale_ids].astype(jnp.float32) + stream_rows).astype(jnp.bfloat16)
    values_in = block_in.astype(jnp.float32)
    normed = (values_in * lax.rsqrt(lax.optimization_barrier(jnp.mean(values_in * values_in, axis=-1, keepdims=True)) + 1e-06) * norm_gain).astype(jnp.bfloat16)
    projected = jnp.dot(normed, qkv_weight, preferred_element_type=jnp.float32).astype(jnp.bfloat16)
    projected = lax.optimization_barrier(projected).astype(jnp.float32)
    queries = projected[:, :width_attn].reshape(-1, HEADS, HEAD_DIM)
    key_mat = projected[:, width_attn:2 * width_attn].reshape(-1, HEADS, HEAD_DIM)
    value_mat = projected[:, 2 * width_attn:].reshape(-1, HEADS, HEAD_DIM)
    scores = jnp.einsum('qhd,khd->hqk', queries, key_mat) * factor
    allowed = scale_ids[None, :] <= scale_ids[:, None]
    scores = jnp.where(allowed[None], scores, -jnp.inf)
    top = lax.optimization_barrier(jnp.max(scores, axis=-1, keepdims=True))
    expd = jnp.exp(scores - top)
    probs = (expd / lax.optimization_barrier(jnp.sum(expd, axis=-1, keepdims=True))).astype(jnp.bfloat16)
    probs = lax.optimization_barrier(probs).astype(jnp.float32)
    attended = jnp.einsum('hqk,khd->qhd', probs, value_mat).reshape(-1, width_attn).astype(jnp.bfloat16)
    mixed = values_in + jnp.dot(attended, out_weight.T, preferred_element_type=jnp.float32)
    block_out = mixed.astype(jnp.bfloat16)
    placed = jnp.zeros((N_TOK * SLOT, D), jnp.bfloat16).at[slots].set(block_out)
    upstream = cotangent[slots]
    out_term = jnp.dot(upstream.T, attended, preferred_element_type=jnp.float32)
    attended_grad = jnp.dot(upstream, out_weight, preferred_element_type=jnp.float32).astype(jnp.bfloat16)
    grad_heads = lax.optimization_barrier(attended_grad).astype(jnp.float32).reshape(-1, HEADS, HEAD_DIM)
    dprobs = jnp.einsum('qhd,khd->hqk', grad_heads, value_mat)
    delta = lax.optimization_barrier(jnp.sum(probs * dprobs, axis=-1, keepdims=True))
    score_grad = (probs * (dprobs - delta) * factor).astype(jnp.bfloat16)
    score_grad = lax.optimization_barrier(score_grad).astype(jnp.float32)
    query_grad = jnp.einsum('hqk,khd->qhd', score_grad, key_mat).reshape(-1, width_attn).astype(jnp.bfloat16)
    key_grad = jnp.einsum('hqk,qhd->khd', score_grad, queries).reshape(-1, width_attn)
    value_grad = jnp.einsum('hqk,qhd->khd', probs, grad_heads).reshape(-1, width_attn)
    kv_grad = jnp.concatenate([key_grad, value_grad], axis=1).astype(jnp.float32)
    query_term = jnp.dot(normed.T, query_grad, preferred_element_type=jnp.float32)
    pair_term = jnp.dot(normed.astype(jnp.float32).T, kv_grad, precision=lax.Precision.HIGHEST)
    qkv_term = jnp.concatenate([query_term, pair_term], axis=1)
    return (placed, qkv_term, out_term)

def reference(residuals, stream, token_slot, level_embed, embed_weight, norm_gain, qkv_weight, out_weight, out_grad):
    width_attn = HEADS * HEAD_DIM

    def one_step(carry, inputs):
        placed, qkv_term, out_term = image_terms(inputs[0], inputs[1], inputs[2], inputs[3], level_embed, embed_weight, norm_gain, qkv_weight, out_weight)
        return ((carry[0] + qkv_term, carry[1] + out_term), placed)
    start_sums = (jnp.zeros((D, 3 * width_attn), jnp.float32), jnp.zeros((D, width_attn), jnp.float32))
    sums, block_out = lax.scan(one_step, start_sums, (residuals, stream, token_slot, out_grad))
    return (block_out, sums[0].reshape(D, 3, width_attn), sums[1])
```

```python
import functools

import jax
import jax.numpy as jnp
import numpy as np
from jax import lax
from jax.experimental import pallas as pl
from jax.experimental.pallas import tpu as pltpu
from jax.sharding import PartitionSpec as P

D = 1024
HEAD_DIM = 128
NSCALE = 7
SLOT = 136
PAD = 144
CHUNK = 48
SLABS = 4
ROWS = SLABS * PAD
COLS = 256
SIDES = (1, 2, 4, 6, 8, 12, 16)
TOK_IMG = 521
TOK_IN = 265
SIZE = {"x": 2, "y": 4, "z": 8}
BLOCKS = ("out", "v", "q", "k")
ORDER = {"out": "yxz", "v": "xyz", "q": "yxz", "k": "xyz"}
PLACE = {"q": 0, "k": 1, "v": 2}
MESH = pl.DeviceIdType.MESH
F32 = jnp.float32
BF16 = jnp.bfloat16


def line_matrix(source, target):
    places = np.arange(target)
    numerator = (2 * places + 1) * source - target
    low_index = numerator // (2 * target)
    fraction = (numerator - low_index * 2 * target) / (2.0 * target)
    fraction = np.where(numerator < 0, 0.0, fraction)
    low_index = np.maximum(low_index, 0)
    fraction = np.where(low_index >= source - 1, 0.0, fraction)
    low_index = np.minimum(low_index, source - 1)
    high_index = np.minimum(low_index + 1, source - 1)
    columns = np.arange(source)
    return (columns[None, :] == low_index[:, None]) * (1.0 - fraction[:, None]) + (
        columns[None, :] == high_index[:, None]
    ) * fraction[:, None]


def teacher_matrix():
    finest = SIDES[-1]
    starts = np.concatenate([[0], np.cumsum([s * s for s in SIDES])])
    whole = np.zeros((TOK_IMG, TOK_IN))
    for k in range(NSCALE - 1):
        down = line_matrix(finest, SIDES[k + 1])
        for j in range(k + 1):
            one = down @ line_matrix(SIDES[j], finest)
            whole[starts[k + 1] : starts[k + 2], starts[j] : starts[j + 1]] = np.kron(one, one)
    return whole.astype(np.float32)


def scale_tables():
    scale = np.repeat(np.arange(NSCALE), [s * s for s in SIDES])
    table = np.zeros((TOK_IMG, 8), np.float32)
    table[np.arange(TOK_IMG), scale] = 1.0
    table[:, 7] = scale - NSCALE
    row = np.zeros((8, TOK_IMG), np.float32)
    row[0] = scale - NSCALE
    return table, row


def dot(a, b, ca=1, cb=0, **kw):
    return lax.dot_general(
        a, b, (((ca,), (cb,)), ((), ())), preferred_element_type=F32, **kw
    )


def kernel(names, *refs):
    r = dict(zip(names, refs, strict=True))
    i, t = lax.axis_index("img"), lax.axis_index("tok")
    core, x_hi = lax.rem(t, 2), lax.div(t, 2)
    mine = {"x": lax.div(i, 32), "y": lax.rem(lax.div(i, 8), 4), "z": lax.rem(i, 8)}

    tok_of = [t, x_hi * 2 + (1 - core), (1 - x_hi) * 2 + core, (1 - x_hi) * 2 + (1 - core)]
    peer = [(i, n) for n in tok_of]

    def along(axis, d):
        at = dict(mine)
        at[axis] = lax.rem(mine[axis] + d, SIZE[axis])
        return ((at["x"] * 4 + at["y"]) * 8 + at["z"], t)

    send, recv = r["send"], r["recv"]
    used = [0]

    def remote(src, dst, device):
        n = used[0]
        used[0] += 1
        return pltpu.make_async_remote_copy(
            src_ref=src,
            dst_ref=dst,
            send_sem=send.at[n],
            recv_sem=recv.at[n],
            device_id=device,
            device_id_type=MESH,
        )

    loads = []
    for s in range(SLABS):
        at = pl.multiple_of(tok_of[s] * COLS, COLS)
        loads.append(
            pltpu.make_async_copy(
                r["out_weight"].at[:, pl.ds(at, COLS)], r["ow"].at[s], r["local"].at[s]
            )
        )
    for b in range(3):
        at = pl.multiple_of(b * D + t * COLS, COLS)
        loads.append(
            pltpu.make_async_copy(
                r["qkv_weight"].at[:, pl.ds(at, COLS)], r["wq"].at[b], r["local"].at[4 + b]
            )
        )
    for load in loads:
        load.start()

    friends = peer[1:] + [along(a, d) for a in "xyz" for d in range(1, SIZE[a])]
    barrier = pltpu.get_barrier_semaphore()
    for f in friends:
        pl.semaphore_signal(barrier, inc=1, device_id=f, device_id_type=MESH)

    none = jnp.zeros((PAD - SLOT, D), F32)
    r["res"][t] = r["residuals"][0]
    r["sbuf"][0] = jnp.concatenate([r["stream"][0].astype(F32), none], 0).astype(BF16)
    r["ubuf"][0] = jnp.concatenate([r["out_grad"][0].astype(F32), none], 0).astype(BF16)
    pl.semaphore_wait(barrier, len(friends))

    res_copies = [remote(r["res"].at[t], r["res"].at[t], peer[s]) for s in (1, 2, 3)]
    pieces = [pl.ds(CHUNK * c, CHUNK) for c in range(PAD // CHUNK)]

    def gather_copies(buf):
        cross = [remote(buf.at[0, p], buf.at[2, p], peer[2]) for p in pieces]
        near = remote(buf.at[0], buf.at[1], peer[1])
        onward = [remote(buf.at[2, p], buf.at[3, p], peer[1]) for p in pieces]
        return cross, near, onward

    s_cross, s_near, s_onward = gather_copies(r["sbuf"])
    u_cross, u_near, u_onward = gather_copies(r["ubuf"])
    for c in res_copies + s_cross + [s_near]:
        c.start()

    row = lax.broadcasted_iota(jnp.int32, (ROWS, 1), 0)
    slot = jnp.full((ROWS, 1), -1, jnp.int32)
    for s in range(SLABS):
        inside = (row >= s * PAD) & (row < s * PAD + SLOT)
        slot = jnp.where(inside, row + (tok_of[s] * SLOT - s * PAD), slot)
    pick = jnp.where(slot == r["token_slot"][...], 1.0, 0.0).astype(BF16)
    levels = dot(pick, r["scale_table"][...])
    sc_col = levels[:, 7:8]
    r["sc_col"][...] = sc_col
    r["sc_row"][...] = dot(r["scale_row"][...], pick, 1, 1)
    for c in res_copies:
        c.wait_recv()
    teacher = dot(
        r["teacher_map"][...],
        r["res"][...].reshape(32, TOK_IN),
        1,
        1,
        precision=lax.Precision.HIGHEST,
    ).astype(BF16)
    r["chan"][...] = dot(pick, teacher).astype(BF16)
    r["lev"][...] = levels[:, :7].astype(BF16)

    def enter(s):
        at = pl.ds(s * PAD, PAD)
        base = dot(r["chan"][at, :], r["embed_weight"][...]) + dot(
            r["lev"][at, :], r["level_embed"][...]
        )
        block_in = (base + r["sbuf"][s].astype(F32)).astype(BF16)
        if s == 0:
            r["block_in"][...] = block_in
        x = block_in.astype(F32)
        scale = lax.rsqrt(jnp.mean(x * x, axis=-1, keepdims=True) + 1e-6)
        r["normed"][at, :] = (x * scale * r["norm_gain"][...]).astype(BF16)

    def project(first):
        at = pl.ds(first * PAD, 2 * PAD)
        for b in range(3):
            r["qkv"][b, at, :] = dot(r["normed"][at, :], r["wq"][b]).astype(BF16)

    enter(0)
    s_near.wait_recv()
    enter(1)
    for load in loads:
        load.wait()
    project(0)
    for c in range(len(pieces)):
        s_cross[c].wait_recv()
        s_onward[c].start()
        u_cross[c].start()
    u_near.start()
    enter(2)
    for c in s_onward:
        c.wait_recv()
    enter(3)
    project(2)

    factor = HEAD_DIM ** (-0.5)
    heads = [slice(h * HEAD_DIM, (h + 1) * HEAD_DIM) for h in range(2)]
    for h in range(2):
        k, v = r["qkv"][1, :, heads[h]], r["qkv"][2, :, heads[h]]
        for s in range(SLABS):
            at = pl.ds(s * PAD, PAD)
            scores = dot(r["qkv"][0, at, heads[h]], k, 1, 1) * factor
            allowed = r["sc_row"][0:1, :] <= r["sc_col"][at, :]
            scores = jnp.where(allowed, scores, -jnp.inf)
            top = jnp.max(scores, axis=-1, keepdims=True)
            expd = jnp.exp(scores - top)
            total = jnp.sum(expd, axis=-1, keepdims=True)
            probs = (expd * (1.0 / total)).astype(BF16)
            r["probs"][h, at, :] = probs
            r["att"][s, :, heads[h]] = dot(probs, v).astype(BF16)

    a_copies = [remote(r["att"].at[s], r["attin"].at[s - 1], peer[s]) for s in (1, 2, 3)]
    for c in a_copies:
        c.start()

    for c in range(len(pieces)):
        u_cross[c].wait_recv()
        u_onward[c].start()
    u_near.wait_recv()
    for c in u_onward:
        c.wait_recv()
    for s in range(SLABS):
        at = pl.ds(s * PAD, PAD)
        up = jnp.where(r["sc_col"][at, :] < 0.0, r["ubuf"][s].astype(F32), 0.0)
        r["up"][at, :] = up.astype(BF16)

    sums = {}

    def first_stage(name, rows_ref, cols):
        order = ORDER[name]
        g = dot(r[rows_ref][...], cols, 0, 0)
        gf, gb = r["gf_" + name], r["gb_" + name]
        for x in range(2):
            for y in range(4):
                part = g[x * 512 + y * 128 : x * 512 + (y + 1) * 128].reshape(8, 16, COLS)
                at = tuple({"x": x, "y": y}[a] for a in order[:2])
                gf[at] = part
                gb[at] = part.astype(BF16)
        return start(name, 0, gb)

    def start(name, stage, src):
        axis = ORDER[name][stage]
        n = SIZE[axis]
        copies = [
            remote(
                src.at[lax.rem(mine[axis] + d, n)],
                r[f"r{stage}_{name}"].at[d - 1],
                along(axis, d),
            )
            for d in range(1, n)
        ]
        for c in copies:
            c.start()
        sums[name, stage] = copies

    def finish(name, stage):
        axis = ORDER[name][stage]
        own = r["gf_" + name] if stage == 0 else r[f"sf{stage - 1}_{name}"]
        for c in sums[name, stage]:
            c.wait_recv()
        total = own[mine[axis]]
        for d in range(1, SIZE[axis]):
            total = total + r[f"r{stage}_{name}"][d - 1].astype(F32)
        if stage < 2:
            r[f"sf{stage}_{name}"][...] = total
            r[f"sb{stage}_{name}"][...] = total.astype(BF16)
            start(name, stage + 1, r[f"sb{stage}_{name}"])
        elif name == "out":
            r["out_weight_grad"][...] = total
        else:
            r["qkv_weight_grad"][:, PLACE[name], :] = total

    att = jnp.concatenate([r["att"][s] for s in range(SLABS)], 0)
    first_stage("out", "up", att)
    r["ag"][...] = dot(r["up"][...], r["ow"][0]).astype(BF16)
    for h in range(2):
        r["dv"][:, heads[h]] = dot(r["probs"][h], r["ag"][:, heads[h]], 0, 0).astype(BF16)
    first_stage("v", "normed", r["dv"][...])
    for h in range(2):
        k, v = r["qkv"][1, :, heads[h]], r["qkv"][2, :, heads[h]]
        for s in range(SLABS):
            at = pl.ds(s * PAD, PAD)
            dprobs = dot(r["ag"][at, heads[h]], v, 1, 1)
            probs = r["probs"][h, at, :].astype(F32)
            delta = jnp.sum(probs * dprobs, axis=-1, keepdims=True)
            ds = (probs * (dprobs - delta) * factor).astype(BF16)
            r["ds"][h, at, :] = ds
            r["dq"][at, heads[h]] = dot(ds, k).astype(BF16)
    first_stage("q", "normed", r["dq"][...])
    for h in range(2):
        r["dk"][:, heads[h]] = dot(r["ds"][h], r["qkv"][0, :, heads[h]], 0, 0).astype(BF16)
    first_stage("k", "normed", r["dk"][...])
    finish("out", 0)

    mixed = r["block_in"][...].astype(F32) + dot(r["att"][0], r["ow"][0], 1, 1)
    for s in (1, 2, 3):
        a_copies[s - 1].wait_recv()
        mixed = mixed + dot(r["attin"][s - 1], r["ow"][s], 1, 1)
    mixed = jnp.where(r["sc_col"][pl.ds(0, PAD), :] < 0.0, mixed, 0.0)
    r["block_out"][0] = mixed[:SLOT].astype(BF16)

    for name in BLOCKS[1:]:
        finish(name, 0)
    for stage in (1, 2):
        for name in BLOCKS:
            finish(name, stage)
    for c in res_copies + s_cross + s_onward + u_cross + u_onward + a_copies + [s_near, u_near]:
        c.wait_send()
    for copies in sums.values():
        for c in copies:
            c.wait_send()


def scratch():
    out = {
        "send": pltpu.SemaphoreType.DMA((68,)),
        "recv": pltpu.SemaphoreType.DMA((68,)),
        "local": pltpu.SemaphoreType.DMA((7,)),
        "ow": pltpu.VMEM((SLABS, D, COLS), BF16),
        "wq": pltpu.VMEM((3, D, COLS), BF16),
        "res": pltpu.VMEM((4, 8, TOK_IN), F32),
        "sbuf": pltpu.VMEM((SLABS, PAD, D), BF16),
        "ubuf": pltpu.VMEM((SLABS, PAD, D), BF16),
        "sc_col": pltpu.VMEM((ROWS, 1), F32),
        "sc_row": pltpu.VMEM((8, ROWS), F32),
        "chan": pltpu.VMEM((ROWS, 32), BF16),
        "lev": pltpu.VMEM((ROWS, 7), BF16),
        "block_in": pltpu.VMEM((PAD, D), BF16),
        "normed": pltpu.VMEM((ROWS, D), BF16),
        "up": pltpu.VMEM((ROWS, D), BF16),
        "qkv": pltpu.VMEM((3, ROWS, COLS), BF16),
        "probs": pltpu.VMEM((2, ROWS, ROWS), BF16),
        "ds": pltpu.VMEM((2, ROWS, ROWS), BF16),
        "att": pltpu.VMEM((SLABS, PAD, COLS), BF16),
        "attin": pltpu.VMEM((SLABS - 1, PAD, COLS), BF16),
        "ag": pltpu.VMEM((ROWS, COLS), BF16),
        "dv": pltpu.VMEM((ROWS, COLS), BF16),
        "dq": pltpu.VMEM((ROWS, COLS), BF16),
        "dk": pltpu.VMEM((ROWS, COLS), BF16),
    }
    for name in BLOCKS:
        n1, n2, n3 = (SIZE[a] for a in ORDER[name])
        out["gf_" + name] = pltpu.VMEM((n1, n2, n3, 16, COLS), F32)
        out["gb_" + name] = pltpu.VMEM((n1, n2, n3, 16, COLS), BF16)
        out["r0_" + name] = pltpu.VMEM((n1 - 1, n2, n3, 16, COLS), BF16)
        out["sf0_" + name] = pltpu.VMEM((n2, n3, 16, COLS), F32)
        out["sb0_" + name] = pltpu.VMEM((n2, n3, 16, COLS), BF16)
        out["r1_" + name] = pltpu.VMEM((n2 - 1, n3, 16, COLS), BF16)
        out["sf1_" + name] = pltpu.VMEM((n3, 16, COLS), F32)
        out["sb1_" + name] = pltpu.VMEM((n3, 16, COLS), BF16)
        out["r2_" + name] = pltpu.VMEM((n3 - 1, 16, COLS), BF16)
    return out


INPUTS = (
    "residuals",
    "stream",
    "token_slot",
    "level_embed",
    "embed_weight",
    "norm_gain",
    "qkv_weight",
    "out_weight",
    "out_grad",
    "teacher_map",
    "scale_table",
    "scale_row",
)
OUTPUTS = ("block_out", "qkv_weight_grad", "out_weight_grad")


def per_device(*args):
    ins = dict(zip(INPUTS, args))
    table, row = scale_tables()
    ins["norm_gain"] = ins["norm_gain"].reshape(1, D)
    ins["teacher_map"] = jnp.asarray(teacher_matrix())
    ins["scale_table"] = jnp.asarray(table, BF16)
    ins["scale_row"] = jnp.asarray(row, BF16)
    buffers = scratch()
    vmem = pl.BlockSpec(memory_space=pltpu.VMEM)
    far = pl.BlockSpec(memory_space=pl.ANY)
    return pl.pallas_call(
        functools.partial(kernel, INPUTS + OUTPUTS + tuple(buffers)),
        out_shape=(
            jax.ShapeDtypeStruct((1, SLOT, D), BF16),
            jax.ShapeDtypeStruct((16, 3, COLS), F32),
            jax.ShapeDtypeStruct((16, COLS), F32),
        ),
        in_specs=[far if n in ("qkv_weight", "out_weight") else vmem for n in INPUTS],
        out_specs=(vmem, vmem, vmem),
        scratch_shapes=list(buffers.values()),
        compiler_params=pltpu.CompilerParams(
            collective_id=0, has_side_effects=True, vmem_limit_bytes=56 << 20
        ),
    )(*[ins[n] for n in INPUTS])


def solution(mesh):
    in_specs = (
        P("img", "tok", None),
        P("img", "tok", None),
        P("img", None),
        P(),
        P(),
        P(),
        P(),
        P(),
        P("img", "tok", None),
    )
    out_specs = (P("img", "tok", None), P("img", None, "tok"), P("img", "tok"))
    return jax.shard_map(
        per_device, mesh=mesh, in_specs=in_specs, out_specs=out_specs, check_vma=False
    )
```

```python
import functools

import jax
import jax.numpy as jnp
import numpy as np
from jax import lax
from jax.experimental import pallas as pl
from jax.experimental.pallas import tpu as pltpu
from jax.sharding import PartitionSpec as P

D = 1024
HEAD_DIM = 128
NSCALE = 7
SLOT = 136
PAD = 144
CHUNK = 48
SLABS = 4
ROWS = SLABS * PAD
COLS = 256
SIDES = (1, 2, 4, 6, 8, 12, 16)
TOK_IMG = 521
TOK_IN = 265
SIZE = {"x": 2, "y": 4, "z": 8}
ORDER = {
    ("out", 0): "zxy",
    ("out", 1): "yxz",
    ("v", 0): "xyz",
    ("v", 1): "yxz",
    ("q", 0): "xyz",
    ("k", 0): "xyz",
    ("q", 1): "zxy",
    ("k", 1): "yxz",
}
FINISH = (
    (("out", 1), 0),
    (("v", 0), 0),
    (("v", 1), 0),
    (("q", 0), 0),
    (("out", 0), 0),
    (("k", 1), 0),
    (("k", 0), 0),
    (("out", 1), 1),
    (("v", 0), 1),
    (("v", 1), 1),
    (("out", 0), 1),
    (("q", 0), 1),
    (("k", 1), 1),
    (("q", 1), 0),
    (("k", 0), 1),
    (("out", 0), 2),
    (("q", 1), 1),
    (("out", 1), 2),
    (("v", 0), 2),
    (("v", 1), 2),
    (("q", 0), 2),
    (("k", 1), 2),
    (("q", 1), 2),
    (("k", 0), 2),
)
PLACE = {"q": 0, "k": 1, "v": 2, "out": 3}
LOADED = ("residuals", "token_slot", "norm_gain", "embed_weight", "teacher_map")
MESH = pl.DeviceIdType.MESH
F32 = jnp.float32
BF16 = jnp.bfloat16


def line_matrix(source, target):
    places = np.arange(target)
    numerator = (2 * places + 1) * source - target
    low_index = numerator // (2 * target)
    fraction = (numerator - low_index * 2 * target) / (2.0 * target)
    fraction = np.where(numerator < 0, 0.0, fraction)
    low_index = np.maximum(low_index, 0)
    fraction = np.where(low_index >= source - 1, 0.0, fraction)
    low_index = np.minimum(low_index, source - 1)
    high_index = np.minimum(low_index + 1, source - 1)
    columns = np.arange(source)
    return (columns[None, :] == low_index[:, None]) * (1.0 - fraction[:, None]) + (
        columns[None, :] == high_index[:, None]
    ) * fraction[:, None]


def teacher_matrix():
    finest = SIDES[-1]
    starts = np.concatenate([[0], np.cumsum([s * s for s in SIDES])])
    whole = np.zeros((TOK_IMG, TOK_IN))
    for k in range(NSCALE - 1):
        down = line_matrix(finest, SIDES[k + 1])
        for j in range(k + 1):
            one = down @ line_matrix(SIDES[j], finest)
            whole[starts[k + 1] : starts[k + 2], starts[j] : starts[j + 1]] = np.kron(one, one)
    return whole.astype(np.float32)


def scale_of(shape, dim):
    token = lax.broadcasted_iota(jnp.int32, shape, dim)
    scale = jnp.full(shape, -NSCALE, jnp.int32)
    for start in np.cumsum([side * side for side in SIDES[:-1]]):
        scale = scale + jnp.where(token >= int(start), 1, 0)
    return scale


def dot(a, b, ca=1, cb=0, **kw):
    return lax.dot_general(
        a, b, (((ca,), (cb,)), ((), ())), preferred_element_type=F32, **kw
    )


def kernel(names, *refs):
    r = dict(zip(names, refs, strict=True))
    i, t = lax.axis_index("img"), lax.axis_index("tok")
    core, x_hi = lax.rem(t, 2), lax.div(t, 2)
    mine = {"x": lax.div(i, 32), "y": lax.rem(lax.div(i, 8), 4), "z": lax.rem(i, 8)}

    tok_of = [t, x_hi * 2 + (1 - core), (1 - x_hi) * 2 + core, (1 - x_hi) * 2 + (1 - core)]
    peer = [(i, n) for n in tok_of]

    def along(axis, d):
        at = dict(mine)
        at[axis] = lax.rem(mine[axis] + d, SIZE[axis])
        return ((at["x"] * 4 + at["y"]) * 8 + at["z"], t)

    send, recv = r["send"], r["recv"]
    used = [0]

    def remote(src, dst, device):
        n = used[0]
        used[0] += 1
        return pltpu.make_async_remote_copy(
            src_ref=src,
            dst_ref=dst,
            send_sem=send.at[n],
            recv_sem=recv.at[n],
            device_id=device,
            device_id_type=MESH,
        )

    loads = []
    for s in range(SLABS):
        at = pl.multiple_of(tok_of[s] * COLS, COLS)
        loads.append(
            pltpu.make_async_copy(
                r["out_weight"].at[:, pl.ds(at, COLS)], r["ow"].at[s], r["local"].at[s]
            )
        )
    for b in range(3):
        at = pl.multiple_of(b * D + t * COLS, COLS)
        loads.append(
            pltpu.make_async_copy(
                r["qkv_weight"].at[:, pl.ds(at, COLS)], r["wq"].at[b], r["local"].at[4 + b]
            )
        )
    small = [
        pltpu.make_async_copy(r[n], r["l_" + n], r["local"].at[7 + k])
        for k, n in enumerate(LOADED)
    ]
    for load in small + loads:
        load.start()

    friends = peer[1:] + [along(a, d) for a in "xyz" for d in range(1, SIZE[a])]
    barrier = pltpu.get_barrier_semaphore()
    for f in friends:
        pl.semaphore_signal(barrier, inc=1, device_id=f, device_id_type=MESH)

    none = jnp.zeros((PAD - SLOT, D), F32)
    r["sbuf"][0] = jnp.concatenate([r["stream"][0].astype(F32), none], 0).astype(BF16)
    r["ubuf"][0] = jnp.concatenate([r["out_grad"][0].astype(F32), none], 0).astype(BF16)
    for load in small:
        load.wait()
    r["res"][t] = r["l_residuals"][0]
    pl.semaphore_wait(barrier, len(friends))

    res_copies = [remote(r["res"].at[t], r["res"].at[t], peer[s]) for s in (1, 2, 3)]
    pieces = [pl.ds(CHUNK * c, CHUNK) for c in range(PAD // CHUNK)]

    def gather_copies(buf):
        cross = [remote(buf.at[0, p], buf.at[2, p], peer[2]) for p in pieces]
        near = remote(buf.at[0], buf.at[1], peer[1])
        onward = [remote(buf.at[2, p], buf.at[3, p], peer[1]) for p in pieces]
        return cross, near, onward

    s_cross, s_near, s_onward = gather_copies(r["sbuf"])
    u_cross, u_near, u_onward = gather_copies(r["ubuf"])
    for c in res_copies + s_cross + [s_near]:
        c.start()

    row = lax.broadcasted_iota(jnp.int32, (ROWS, 1), 0)
    slot = jnp.full((ROWS, 1), -1, jnp.int32)
    for s in range(SLABS):
        inside = (row >= s * PAD) & (row < s * PAD + SLOT)
        slot = jnp.where(inside, row + (tok_of[s] * SLOT - s * PAD), slot)
    pick = jnp.where(slot == r["l_token_slot"][...], 1.0, 0.0).astype(BF16)
    lane = lax.broadcasted_iota(jnp.int32, (TOK_IMG, 8), 1)
    scale = scale_of((TOK_IMG, 8), 0)
    table = jnp.where(lane == scale + NSCALE, 1, 0) + jnp.where(lane == 7, scale, 0)
    levels = dot(pick, table.astype(F32).astype(BF16))
    sc_col = levels[:, 7:8]
    r["sc_col"][...] = sc_col
    r["sc_row"][...] = dot(
        scale_of((8, TOK_IMG), 1).astype(F32).astype(BF16), pick, 1, 1
    )
    for c in res_copies:
        c.wait_recv()
    teacher = dot(
        r["l_teacher_map"][...],
        r["res"][...].reshape(32, TOK_IN),
        1,
        1,
        precision=lax.Precision.HIGHEST,
    ).astype(BF16)
    r["chan"][...] = dot(pick, teacher).astype(BF16)
    r["lev"][...] = levels[:, :7].astype(BF16)

    def enter(s):
        at = pl.ds(s * PAD, PAD)
        base = dot(r["chan"][at, :], r["l_embed_weight"][...]) + dot(
            r["lev"][at, :], r["level_embed"][...]
        )
        block_in = (base + r["sbuf"][s].astype(F32)).astype(BF16)
        if s == 0:
            r["block_in"][...] = block_in
        x = block_in.astype(F32)
        scale = lax.rsqrt(jnp.mean(x * x, axis=-1, keepdims=True) + 1e-6)
        r["normed"][at, :] = (x * scale * r["l_norm_gain"][...]).astype(BF16)

    def project(first):
        at = pl.ds(first * PAD, 2 * PAD)
        for b in range(3):
            r["qkv"][b, at, :] = dot(r["normed"][at, :], r["wq"][b]).astype(BF16)

    enter(0)
    s_near.wait_recv()
    enter(1)
    for load in loads:
        load.wait()
    project(0)
    for c in range(len(pieces)):
        s_cross[c].wait_recv()
        s_onward[c].start()
        u_cross[c].start()
    u_near.start()
    enter(2)
    for c in s_onward:
        c.wait_recv()
    enter(3)
    project(2)
    r["normed_t"][...] = r["normed"][...].T

    factor = HEAD_DIM ** (-0.5)
    heads = [slice(h * HEAD_DIM, (h + 1) * HEAD_DIM) for h in range(2)]
    for h in range(2):
        k, v = r["qkv"][1, :, heads[h]], r["qkv"][2, :, heads[h]]
        for s in range(SLABS):
            at = pl.ds(s * PAD, PAD)
            scores = dot(r["qkv"][0, at, heads[h]], k, 1, 1) * factor
            allowed = r["sc_row"][0:1, :] <= r["sc_col"][at, :]
            scores = jnp.where(allowed, scores, -jnp.inf)
            top = jnp.max(scores, axis=-1, keepdims=True)
            expd = jnp.exp(scores - top)
            total = jnp.sum(expd, axis=-1, keepdims=True)
            probs = (expd * (1.0 / total)).astype(BF16)
            r["probs"][h, at, :] = probs
            r["att"][s, :, heads[h]] = dot(probs, v).astype(BF16)

    for c in range(len(pieces)):
        u_cross[c].wait_recv()
        u_onward[c].start()
    a_copies = [remote(r["att"].at[s], r["attin"].at[s - 1], peer[s]) for s in (1, 2, 3)]
    for c in a_copies:
        c.start()
    u_near.wait_recv()
    for c in u_onward:
        c.wait_recv()
    for s in range(SLABS):
        at = pl.ds(s * PAD, PAD)
        up = jnp.where(r["sc_col"][at, :] < 0.0, r["ubuf"][s].astype(F32), 0.0)
        r["up"][at, :] = up.astype(BF16)

    sums = {}

    def first_stage(names, g):
        for n, name in enumerate(names):
            order, gf, gb = ORDER[name], r["gf", name], r["gb", name]
            for x in range(2):
                for y in range(4):
                    rows = slice(x * 512 + y * 128, x * 512 + (y + 1) * 128)
                    part = g[rows, heads[n]].reshape(8, 16, HEAD_DIM)
                    at = tuple({"x": x, "y": y, "z": slice(None)}[a] for a in order)
                    gf[at] = part
                    gb[at] = part.astype(BF16)
            start(name, 0, gb)

    def start(name, stage, src):
        axis = ORDER[name][stage]
        n = SIZE[axis]
        copies = [
            remote(
                src.at[lax.rem(mine[axis] + d, n)],
                r["in", stage, name].at[d - 1],
                along(axis, d),
            )
            for d in range(1, n)
        ]
        for c in copies:
            c.start()
        sums[name, stage] = copies

    def finish(name, stage):
        axis = ORDER[name][stage]
        own = r["gf", name] if stage == 0 else r["sf", stage - 1, name]
        for c in sums[name, stage]:
            c.wait_recv()
        total = own[mine[axis]]
        for d in range(1, SIZE[axis]):
            total = total + r["in", stage, name][d - 1].astype(F32)
        if stage < 2:
            r["sf", stage, name][...] = total
            r["sb", stage, name][...] = total.astype(BF16)
            start(name, stage + 1, r["sb", stage, name])
        else:
            r["weight_grad"][PLACE[name[0]], :, heads[name[1]]] = total

    att = jnp.concatenate([r["att"][s] for s in range(SLABS)], 0)
    first_stage((("out", 0), ("out", 1)), dot(r["up"][...], att, 0, 0))
    r["ag"][...] = dot(r["up"][...], r["ow"][0]).astype(BF16)
    for h in range(2):
        r["dv"][:, heads[h]] = dot(r["probs"][h], r["ag"][:, heads[h]], 0, 0).astype(BF16)
    first_stage((("v", 0), ("v", 1)), dot(r["normed_t"][...], r["dv"][...]))
    for h in range(2):
        k, v = r["qkv"][1, :, heads[h]], r["qkv"][2, :, heads[h]]
        for s in range(SLABS):
            at = pl.ds(s * PAD, PAD)
            dprobs = dot(r["ag"][at, heads[h]], v, 1, 1)
            probs = r["probs"][h, at, :].astype(F32)
            delta = jnp.sum(probs * dprobs, axis=-1, keepdims=True)
            ds = (probs * (dprobs - delta) * factor).astype(BF16)
            r["ds"][h, at, :] = ds
            r["dqk"][at, heads[0]] = dot(ds, k).astype(BF16)
        r["dqk"][:, heads[1]] = dot(r["ds"][h], r["qkv"][0, :, heads[h]], 0, 0).astype(BF16)
        first_stage((("q", h), ("k", h)), dot(r["normed_t"][...], r["dqk"][...]))

    mixed = r["block_in"][...].astype(F32) + dot(r["att"][0], r["ow"][0], 1, 1)
    for s in (1, 2, 3):
        a_copies[s - 1].wait_recv()
        mixed = mixed + dot(r["attin"][s - 1], r["ow"][s], 1, 1)
    mixed = jnp.where(r["sc_col"][pl.ds(0, PAD), :] < 0.0, mixed, 0.0)
    r["block_out"][0] = mixed[:SLOT].astype(BF16)

    for name, stage in FINISH:
        finish(name, stage)
    for c in res_copies + s_cross + s_onward + u_cross + u_onward + a_copies + [s_near, u_near]:
        c.wait_send()
    for copies in sums.values():
        for c in copies:
            c.wait_send()


def scratch():
    out = {
        "send": pltpu.SemaphoreType.DMA((112,)),
        "recv": pltpu.SemaphoreType.DMA((112,)),
        "local": pltpu.SemaphoreType.DMA((7 + len(LOADED),)),
        "ow": pltpu.VMEM((SLABS, D, COLS), BF16),
        "wq": pltpu.VMEM((3, D, COLS), BF16),
        "res": pltpu.VMEM((4, 8, TOK_IN), F32),
        "sbuf": pltpu.VMEM((SLABS, PAD, D), BF16),
        "ubuf": pltpu.VMEM((SLABS, PAD, D), BF16),
        "sc_col": pltpu.VMEM((ROWS, 1), F32),
        "sc_row": pltpu.VMEM((8, ROWS), F32),
        "chan": pltpu.VMEM((ROWS, 32), BF16),
        "lev": pltpu.VMEM((ROWS, 7), BF16),
        "block_in": pltpu.VMEM((PAD, D), BF16),
        "normed": pltpu.VMEM((ROWS, D), BF16),
        "up": pltpu.VMEM((ROWS, D), BF16),
        "qkv": pltpu.VMEM((3, ROWS, COLS), BF16),
        "probs": pltpu.VMEM((2, ROWS, ROWS), BF16),
        "ds": pltpu.VMEM((2, ROWS, ROWS), BF16),
        "att": pltpu.VMEM((SLABS, PAD, COLS), BF16),
        "attin": pltpu.VMEM((SLABS - 1, PAD, COLS), BF16),
        "ag": pltpu.VMEM((ROWS, COLS), BF16),
        "dv": pltpu.VMEM((ROWS, COLS), BF16),
        "dqk": pltpu.VMEM((ROWS, COLS), BF16),
        "normed_t": pltpu.VMEM((D, ROWS), BF16),
        "l_residuals": pltpu.VMEM((1, 8, TOK_IN), F32),
        "l_token_slot": pltpu.VMEM((1, TOK_IMG), jnp.int32),
        "l_norm_gain": pltpu.VMEM((1, D), F32),
        "l_embed_weight": pltpu.VMEM((32, D), BF16),
        "l_teacher_map": pltpu.VMEM((TOK_IMG, TOK_IN), F32),
    }
    for name, order in ORDER.items():
        n1, n2, n3 = (SIZE[a] for a in order)
        tail = (16, HEAD_DIM)
        out["gf", name] = pltpu.VMEM((n1, n2, n3) + tail, F32)
        out["gb", name] = pltpu.VMEM((n1, n2, n3) + tail, BF16)
        out["in", 0, name] = pltpu.VMEM((n1 - 1, n2, n3) + tail, BF16)
        out["sf", 0, name] = pltpu.VMEM((n2, n3) + tail, F32)
        out["sb", 0, name] = pltpu.VMEM((n2, n3) + tail, BF16)
        out["in", 1, name] = pltpu.VMEM((n2 - 1, n3) + tail, BF16)
        out["sf", 1, name] = pltpu.VMEM((n3,) + tail, F32)
        out["sb", 1, name] = pltpu.VMEM((n3,) + tail, BF16)
        out["in", 2, name] = pltpu.VMEM((n3 - 1,) + tail, BF16)
    return out


def hand_over(block_in, weight_in, block_out, qkv_out, out_out):
    block_out[...] = block_in[...]
    qkv_out[...] = weight_in[:3]
    out_out[...] = weight_in[3]


INPUTS = (
    "residuals",
    "stream",
    "token_slot",
    "level_embed",
    "embed_weight",
    "norm_gain",
    "qkv_weight",
    "out_weight",
    "out_grad",
    "teacher_map",
)
OUTPUTS = ("block_out", "weight_grad")
HELD = ("stream", "out_grad", "level_embed")


def per_device(*args):
    ins = dict(zip(INPUTS, args))
    ins["norm_gain"] = ins["norm_gain"].reshape(1, D)
    ins["teacher_map"] = jnp.asarray(teacher_matrix())
    buffers = scratch()
    vmem = pl.BlockSpec(memory_space=pltpu.VMEM)
    far = pl.BlockSpec(memory_space=pl.ANY)
    block_shape = jax.ShapeDtypeStruct((1, SLOT, D), BF16)
    block_out, weight_grad = pl.pallas_call(
        functools.partial(kernel, INPUTS + OUTPUTS + tuple(buffers)),
        out_shape=(block_shape, jax.ShapeDtypeStruct((4, 16, COLS), F32)),
        in_specs=[vmem if n in HELD else far for n in INPUTS],
        out_specs=(vmem, vmem),
        scratch_shapes=list(buffers.values()),
        compiler_params=pltpu.CompilerParams(
            collective_id=0, has_side_effects=True, vmem_limit_bytes=56 << 20
        ),
    )(*[ins[n] for n in INPUTS])
    block_out, qkv_grad, out_grad = pl.pallas_call(
        hand_over,
        out_shape=(
            block_shape,
            jax.ShapeDtypeStruct((3, 16, COLS), F32),
            jax.ShapeDtypeStruct((16, COLS), F32),
        ),
        in_specs=[vmem] * 2,
        out_specs=(vmem,) * 3,
    )(block_out, weight_grad)
    return block_out, qkv_grad.transpose(1, 0, 2), out_grad


def solution(mesh):
    in_specs = (
        P("img", "tok", None),
        P("img", "tok", None),
        P("img", None),
        P(),
        P(),
        P(),
        P(),
        P(),
        P("img", "tok", None),
    )
    out_specs = (P("img", "tok", None), P("img", None, "tok"), P("img", "tok"))
    return jax.shard_map(
        per_device, mesh=mesh, in_specs=in_specs, out_specs=out_specs, check_vma=False
    )
```

```python
import functools

import jax
import jax.numpy as jnp
import numpy as np
from jax import lax
from jax.experimental import pallas as pl
from jax.experimental.pallas import tpu as pltpu
from jax.sharding import PartitionSpec as P

D = 1024
HEAD_DIM = 128
NSCALE = 7
SLOT = 136
PAD = 144
CHUNK = 48
SLABS = 4
ROWS = SLABS * PAD
COLS = 256
SIDES = (1, 2, 4, 6, 8, 12, 16)
TOK_IMG = 521
TOK_IN = 265
SIZE = {"x": 2, "y": 4, "z": 8}
ORDER = {
    ("out", 0): "zxy",
    ("out", 1): "yxz",
    ("v", 0): "xyz",
    ("v", 1): "yxz",
    ("q", 0): "xyz",
    ("k", 0): "xyz",
    ("q", 1): "zxy",
    ("k", 1): "yxz",
}
FINISH = (
    (("out", 1), 0),
    (("v", 0), 0),
    (("v", 1), 0),
    (("q", 0), 0),
    (("out", 0), 0),
    (("k", 1), 0),
    (("k", 0), 0),
    (("out", 1), 1),
    (("v", 0), 1),
    (("v", 1), 1),
    (("out", 0), 1),
    (("q", 0), 1),
    (("k", 1), 1),
    (("q", 1), 0),
    (("k", 0), 1),
    (("out", 0), 2),
    (("q", 1), 1),
    (("out", 1), 2),
    (("v", 0), 2),
    (("v", 1), 2),
    (("q", 0), 2),
    (("k", 1), 2),
    (("q", 1), 2),
    (("k", 0), 2),
)
PLACE = {"q": 0, "k": 1, "v": 2, "out": 3}
LOADED = (
    "stream",
    "residuals",
    "token_slot",
    "norm_gain",
    "embed_weight",
    "teacher_map",
    "out_grad",
)
MESH = pl.DeviceIdType.MESH
F32 = jnp.float32
BF16 = jnp.bfloat16


def line_matrix(source, target):
    places = np.arange(target)
    numerator = (2 * places + 1) * source - target
    low_index = numerator // (2 * target)
    fraction = (numerator - low_index * 2 * target) / (2.0 * target)
    fraction = np.where(numerator < 0, 0.0, fraction)
    low_index = np.maximum(low_index, 0)
    fraction = np.where(low_index >= source - 1, 0.0, fraction)
    low_index = np.minimum(low_index, source - 1)
    high_index = np.minimum(low_index + 1, source - 1)
    columns = np.arange(source)
    return (columns[None, :] == low_index[:, None]) * (1.0 - fraction[:, None]) + (
        columns[None, :] == high_index[:, None]
    ) * fraction[:, None]


def teacher_matrix():
    finest = SIDES[-1]
    starts = np.concatenate([[0], np.cumsum([s * s for s in SIDES])])
    whole = np.zeros((TOK_IMG, TOK_IN))
    for k in range(NSCALE - 1):
        down = line_matrix(finest, SIDES[k + 1])
        for j in range(k + 1):
            one = down @ line_matrix(SIDES[j], finest)
            whole[starts[k + 1] : starts[k + 2], starts[j] : starts[j + 1]] = np.kron(one, one)
    return whole.astype(np.float32)


def scale_of(shape, dim):
    token = lax.broadcasted_iota(jnp.int32, shape, dim)
    scale = jnp.full(shape, -NSCALE, jnp.int32)
    for start in np.cumsum([side * side for side in SIDES[:-1]]):
        scale = scale + jnp.where(token >= int(start), 1, 0)
    return scale


def dot(a, b, ca=1, cb=0, **kw):
    return lax.dot_general(
        a, b, (((ca,), (cb,)), ((), ())), preferred_element_type=F32, **kw
    )


def kernel(names, *refs):
    r = dict(zip(names, refs, strict=True))
    i, t = lax.axis_index("img"), lax.axis_index("tok")
    core, x_hi = lax.rem(t, 2), lax.div(t, 2)
    mine = {"x": lax.div(i, 32), "y": lax.rem(lax.div(i, 8), 4), "z": lax.rem(i, 8)}

    tok_of = [t, x_hi * 2 + (1 - core), (1 - x_hi) * 2 + core, (1 - x_hi) * 2 + (1 - core)]
    peer = [(i, n) for n in tok_of]

    def along(axis, d):
        at = dict(mine)
        at[axis] = lax.rem(mine[axis] + d, SIZE[axis])
        return ((at["x"] * 4 + at["y"]) * 8 + at["z"], t)

    friends = peer[1:] + [along(a, d) for a in "xyz" for d in range(1, SIZE[a])]
    barrier = pltpu.get_barrier_semaphore()
    for f in friends:
        pl.semaphore_signal(barrier, inc=1, device_id=f, device_id_type=MESH)

    sems, used = r["sems"], [0]

    def new_sem():
        used[0] += 1
        return sems.at[used[0] - 1]

    def remote(src, dst, device, send_sem, recv_sem):
        return pltpu.make_async_remote_copy(
            src_ref=src,
            dst_ref=dst,
            send_sem=send_sem,
            recv_sem=recv_sem,
            device_id=device,
            device_id_type=MESH,
        )

    def wait_bytes(ref, sem):
        pltpu.make_async_copy(ref, ref, sem).wait()

    small = {n: pltpu.make_async_copy(r[n], r["l_" + n], new_sem()) for n in LOADED}
    ow_sem, wq_sem = new_sem(), new_sem()
    loads = []
    for s in range(SLABS):
        at = pl.multiple_of(tok_of[s] * COLS, COLS)
        loads.append(
            pltpu.make_async_copy(r["out_weight"].at[:, pl.ds(at, COLS)], r["ow"].at[s], ow_sem)
        )
    for b in range(3):
        at = pl.multiple_of(b * D + t * COLS, COLS)
        loads.append(
            pltpu.make_async_copy(r["qkv_weight"].at[:, pl.ds(at, COLS)], r["wq"].at[b], wq_sem)
        )
    for load in list(small.values()) + loads:
        load.start()

    none = jnp.zeros((PAD - SLOT, D), F32)
    small["stream"].wait()
    r["sbuf"][0] = jnp.concatenate([r["l_stream"][0].astype(F32), none], 0).astype(BF16)
    small["residuals"].wait()
    r["res"][t] = r["l_residuals"][0]
    pl.semaphore_wait(barrier, len(friends))

    res_copies = [
        remote(r["res"].at[t], r["res"].at[t], peer[s], new_sem(), new_sem()) for s in (1, 2, 3)
    ]
    pieces = [pl.ds(CHUNK * c, CHUNK) for c in range(PAD // CHUNK)]

    def gather_copies(buf):
        sent, onward_sem = new_sem(), new_sem()
        cross = [remote(buf.at[0, p], buf.at[2, p], peer[2], sent, new_sem()) for p in pieces]
        near = remote(buf.at[0], buf.at[1], peer[1], sent, new_sem())
        onward = [remote(buf.at[2, p], buf.at[3, p], peer[1], sent, onward_sem) for p in pieces]
        return cross, near, onward, sent, onward_sem

    s_cross, s_near, s_onward, s_sent, s_onward_sem = gather_copies(r["sbuf"])
    u_cross, u_near, u_onward, u_sent, u_onward_sem = gather_copies(r["ubuf"])
    for c in res_copies + s_cross + [s_near]:
        c.start()
    for n in LOADED[2:]:
        small[n].wait()
    r["ubuf"][0] = jnp.concatenate([r["l_out_grad"][0].astype(F32), none], 0).astype(BF16)

    row = lax.broadcasted_iota(jnp.int32, (ROWS, 1), 0)
    slot = jnp.full((ROWS, 1), -1, jnp.int32)
    for s in range(SLABS):
        inside = (row >= s * PAD) & (row < s * PAD + SLOT)
        slot = jnp.where(inside, row + (tok_of[s] * SLOT - s * PAD), slot)
    pick = jnp.where(slot == r["l_token_slot"][...], 1.0, 0.0).astype(BF16)
    lane = lax.broadcasted_iota(jnp.int32, (TOK_IMG, 8), 1)
    scale = scale_of((TOK_IMG, 8), 0)
    table = jnp.where(lane == scale + NSCALE, 1, 0) + jnp.where(lane == 7, scale, 0)
    levels = dot(pick, table.astype(F32).astype(BF16))
    sc_col = levels[:, 7:8]
    r["sc_col"][...] = sc_col
    r["sc_row"][...] = dot(
        scale_of((8, TOK_IMG), 1).astype(F32).astype(BF16), pick, 1, 1
    )
    for c in res_copies:
        c.wait_recv()
    teacher = dot(
        r["l_teacher_map"][...],
        r["res"][...].reshape(32, TOK_IN),
        1,
        1,
        precision=lax.Precision.HIGHEST,
    ).astype(BF16)
    r["chan"][...] = dot(pick, teacher).astype(BF16)
    r["lev"][...] = levels[:, :7].astype(BF16)

    def enter(s):
        at = pl.ds(s * PAD, PAD)
        base = dot(r["chan"][at, :], r["l_embed_weight"][...]) + dot(
            r["lev"][at, :], r["level_embed"][...]
        )
        block_in = (base + r["sbuf"][s].astype(F32)).astype(BF16)
        if s == 0:
            r["block_in"][...] = block_in
        x = block_in.astype(F32)
        scale = lax.rsqrt(jnp.mean(x * x, axis=-1, keepdims=True) + 1e-6)
        r["normed"][at, :] = (x * scale * r["l_norm_gain"][...]).astype(BF16)

    def project(first):
        at = pl.ds(first * PAD, 2 * PAD)
        for b in range(3):
            r["qkv"][b, at, :] = dot(r["normed"][at, :], r["wq"][b]).astype(BF16)

    enter(0)
    s_near.wait_recv()
    enter(1)
    wait_bytes(r["ow"], ow_sem)
    wait_bytes(r["wq"], wq_sem)
    project(0)
    for c in range(len(pieces)):
        s_cross[c].wait_recv()
        s_onward[c].start()
        u_cross[c].start()
    u_near.start()
    enter(2)
    wait_bytes(r["sbuf"].at[3], s_onward_sem)
    enter(3)
    project(2)
    r["normed_t"][...] = r["normed"][...].T

    factor = HEAD_DIM ** (-0.5)
    heads = [slice(h * HEAD_DIM, (h + 1) * HEAD_DIM) for h in range(2)]
    for h in range(2):
        k, v = r["qkv"][1, :, heads[h]], r["qkv"][2, :, heads[h]]
        for s in range(SLABS):
            at = pl.ds(s * PAD, PAD)
            scores = dot(r["qkv"][0, at, heads[h]], k, 1, 1) * factor
            allowed = r["sc_row"][0:1, :] <= r["sc_col"][at, :]
            scores = jnp.where(allowed, scores, -jnp.inf)
            top = jnp.max(scores, axis=-1, keepdims=True)
            expd = jnp.exp(scores - top)
            total = jnp.sum(expd, axis=-1, keepdims=True)
            probs = (expd * (1.0 / total)).astype(BF16)
            r["probs"][h, at, :] = probs
            r["att"][s, :, heads[h]] = dot(probs, v).astype(BF16)

    for c in range(len(pieces)):
        u_cross[c].wait_recv()
        u_onward[c].start()
    a_sent, a_come = new_sem(), new_sem()
    for s in (1, 2, 3):
        remote(r["att"].at[s], r["attin"].at[s - 1], peer[s], a_sent, a_come).start()
    u_near.wait_recv()
    wait_bytes(r["ubuf"].at[3], u_onward_sem)
    for s in range(SLABS):
        at = pl.ds(s * PAD, PAD)
        up = jnp.where(r["sc_col"][at, :] < 0.0, r["ubuf"][s].astype(F32), 0.0)
        r["up"][at, :] = up.astype(BF16)

    piece_sent, arrival = {}, {}

    def tiles(name, stage):
        sizes = [SIZE[a] for a in ORDER[name]]
        share = (64, 32, 16, 8, 4, 2, 1)[sum(n.bit_length() - 1 for n in sizes[: stage + 1])]
        first = 64 - share * sizes[stage]
        return sizes[stage], share, first

    def first_stage(names, g):
        for n, name in enumerate(names):
            order, gf, gb = ORDER[name], r["gf", name], r["gb", name]
            _, n2, n3 = (SIZE[a] for a in order)
            step = {order[0]: n2 * n3, order[1]: n3, order[2]: 1}
            for x in range(2):
                for y in range(4):
                    rows = slice(x * 512 + y * 128, x * 512 + (y + 1) * 128)
                    part = g[rows, heads[n]].reshape(8, 16, HEAD_DIM)
                    at = x * step["x"] + y * step["y"]
                    if step["z"] == 1:
                        gf[at : at + 8] = part
                        gb[at : at + 8] = part.astype(BF16)
                    else:
                        for z in range(8):
                            gf[at + z * step["z"]] = part[z]
                            gb[at + z * step["z"]] = part[z].astype(BF16)
            piece_sent[name] = new_sem()
            start(name, 0, gb)

    def start(name, stage, src):
        axis = ORDER[name][stage]
        n, share, first = tiles(name, stage)
        arrival[name, stage] = new_sem()
        for d in range(1, n):
            remote(
                src.at[pl.ds(lax.rem(mine[axis] + d, n) * share, share)],
                r["in", name].at[pl.ds(first + (d - 1) * share, share)],
                along(axis, d),
                piece_sent[name],
                arrival[name, stage],
            ).start()

    def finish(name, stage):
        axis = ORDER[name][stage]
        n, share, first = tiles(name, stage)
        come = r["in", name]
        wait_bytes(come.at[pl.ds(first, (n - 1) * share)], arrival[name, stage])
        own = r["gf", name] if stage == 0 else r["sf", stage - 1, name]
        total = own[pl.ds(mine[axis] * share, share)]
        for d in range(1, n):
            total = total + come[pl.ds(first + (d - 1) * share, share)].astype(F32)
        if stage < 2:
            r["sf", stage, name][...] = total
            r["sb", stage, name][...] = total.astype(BF16)
            start(name, stage + 1, r["sb", stage, name])
        else:
            r["weight_grad"][PLACE[name[0]], :, heads[name[1]]] = total[0]

    att = jnp.concatenate([r["att"][s] for s in range(SLABS)], 0)
    first_stage((("out", 0), ("out", 1)), dot(r["up"][...], att, 0, 0))
    r["ag"][...] = dot(r["up"][...], r["ow"][0]).astype(BF16)
    for h in range(2):
        r["dv"][:, heads[h]] = dot(r["probs"][h], r["ag"][:, heads[h]], 0, 0).astype(BF16)
    first_stage((("v", 0), ("v", 1)), dot(r["normed_t"][...], r["dv"][...]))
    for h in range(2):
        k, v = r["qkv"][1, :, heads[h]], r["qkv"][2, :, heads[h]]
        for s in range(SLABS):
            at = pl.ds(s * PAD, PAD)
            dprobs = dot(r["ag"][at, heads[h]], v, 1, 1)
            probs = r["probs"][h, at, :].astype(F32)
            delta = jnp.sum(probs * dprobs, axis=-1, keepdims=True)
            ds = (probs * (dprobs - delta) * factor).astype(BF16)
            r["ds"][h, at, :] = ds
            r["dqk"][at, heads[0]] = dot(ds, k).astype(BF16)
        r["dqk"][:, heads[1]] = dot(r["ds"][h], r["qkv"][0, :, heads[h]], 0, 0).astype(BF16)
        first_stage((("q", h), ("k", h)), dot(r["normed_t"][...], r["dqk"][...]))

    wait_bytes(r["attin"], a_come)
    mixed = r["block_in"][...].astype(F32) + dot(r["att"][0], r["ow"][0], 1, 1)
    for s in (1, 2, 3):
        mixed = mixed + dot(r["attin"][s - 1], r["ow"][s], 1, 1)
    mixed = jnp.where(r["sc_col"][pl.ds(0, PAD), :] < 0.0, mixed, 0.0)
    r["block_out"][0] = mixed[:SLOT].astype(BF16)

    for name, stage in FINISH:
        finish(name, stage)
    for c in res_copies:
        c.wait_send()
    wait_bytes(r["sbuf"].at[pl.ds(1, 3)], s_sent)
    wait_bytes(r["ubuf"].at[pl.ds(1, 3)], u_sent)
    wait_bytes(r["attin"], a_sent)
    for name in ORDER:
        wait_bytes(r["in", name], piece_sent[name])


def scratch():
    out = {
        "sems": pltpu.SemaphoreType.DMA((len(LOADED) + 2 + 6 + 12 + 2 + 32,)),
        "ow": pltpu.VMEM((SLABS, D, COLS), BF16),
        "wq": pltpu.VMEM((3, D, COLS), BF16),
        "res": pltpu.VMEM((4, 8, TOK_IN), F32),
        "sbuf": pltpu.VMEM((SLABS, PAD, D), BF16),
        "ubuf": pltpu.VMEM((SLABS, PAD, D), BF16),
        "sc_col": pltpu.VMEM((ROWS, 1), F32),
        "sc_row": pltpu.VMEM((8, ROWS), F32),
        "chan": pltpu.VMEM((ROWS, 32), BF16),
        "lev": pltpu.VMEM((ROWS, 7), BF16),
        "block_in": pltpu.VMEM((PAD, D), BF16),
        "normed": pltpu.VMEM((ROWS, D), BF16),
        "up": pltpu.VMEM((ROWS, D), BF16),
        "qkv": pltpu.VMEM((3, ROWS, COLS), BF16),
        "probs": pltpu.VMEM((2, ROWS, ROWS), BF16),
        "ds": pltpu.VMEM((2, ROWS, ROWS), BF16),
        "att": pltpu.VMEM((SLABS, PAD, COLS), BF16),
        "attin": pltpu.VMEM((SLABS - 1, PAD, COLS), BF16),
        "ag": pltpu.VMEM((ROWS, COLS), BF16),
        "dv": pltpu.VMEM((ROWS, COLS), BF16),
        "dqk": pltpu.VMEM((ROWS, COLS), BF16),
        "normed_t": pltpu.VMEM((D, ROWS), BF16),
        "l_stream": pltpu.VMEM((1, SLOT, D), BF16),
        "l_out_grad": pltpu.VMEM((1, SLOT, D), BF16),
        "l_residuals": pltpu.VMEM((1, 8, TOK_IN), F32),
        "l_token_slot": pltpu.VMEM((1, TOK_IMG), jnp.int32),
        "l_norm_gain": pltpu.VMEM((1, D), F32),
        "l_embed_weight": pltpu.VMEM((32, D), BF16),
        "l_teacher_map": pltpu.VMEM((TOK_IMG, TOK_IN), F32),
    }
    for name, order in ORDER.items():
        _, n2, n3 = (SIZE[a] for a in order)
        tail = (16, HEAD_DIM)
        out["gf", name] = pltpu.VMEM((64,) + tail, F32)
        out["gb", name] = pltpu.VMEM((64,) + tail, BF16)
        out["in", name] = pltpu.VMEM((63,) + tail, BF16)
        for stage, share in ((0, n2 * n3), (1, n3)):
            out["sf", stage, name] = pltpu.VMEM((share,) + tail, F32)
            out["sb", stage, name] = pltpu.VMEM((share,) + tail, BF16)
    return out


def hand_over(block_in, weight_in, block_out, qkv_out, out_out):
    block_out[...] = block_in[...]
    qkv_out[...] = weight_in[:3]
    out_out[...] = weight_in[3]


INPUTS = (
    "residuals",
    "stream",
    "token_slot",
    "level_embed",
    "embed_weight",
    "norm_gain",
    "qkv_weight",
    "out_weight",
    "out_grad",
    "teacher_map",
)
OUTPUTS = ("block_out", "weight_grad")
HELD = ("level_embed",)


def per_device(*args):
    ins = dict(zip(INPUTS, args))
    ins["norm_gain"] = ins["norm_gain"].reshape(1, D)
    ins["teacher_map"] = jnp.asarray(teacher_matrix())
    buffers = scratch()
    vmem = pl.BlockSpec(memory_space=pltpu.VMEM)
    far = pl.BlockSpec(memory_space=pl.ANY)
    block_shape = jax.ShapeDtypeStruct((1, SLOT, D), BF16)
    block_out, weight_grad = pl.pallas_call(
        functools.partial(kernel, INPUTS + OUTPUTS + tuple(buffers)),
        out_shape=(block_shape, jax.ShapeDtypeStruct((4, 16, COLS), F32)),
        in_specs=[vmem if n in HELD else far for n in INPUTS],
        out_specs=(vmem, vmem),
        scratch_shapes=list(buffers.values()),
        compiler_params=pltpu.CompilerParams(
            collective_id=0, has_side_effects=True, vmem_limit_bytes=56 << 20
        ),
    )(*[ins[n] for n in INPUTS])
    block_out, qkv_grad, out_grad = pl.pallas_call(
        hand_over,
        out_shape=(
            block_shape,
            jax.ShapeDtypeStruct((3, 16, COLS), F32),
            jax.ShapeDtypeStruct((16, COLS), F32),
        ),
        in_specs=[vmem] * 2,
        out_specs=(vmem,) * 3,
    )(block_out, weight_grad)
    return block_out, qkv_grad.transpose(1, 0, 2), out_grad


def solution(mesh):
    in_specs = (
        P("img", "tok", None),
        P("img", "tok", None),
        P("img", None),
        P(),
        P(),
        P(),
        P(),
        P(),
        P("img", "tok", None),
    )
    out_specs = (P("img", "tok", None), P("img", None, "tok"), P("img", "tok"))
    return jax.shard_map(
        per_device, mesh=mesh, in_specs=in_specs, out_specs=out_specs, check_vma=False
    )
```

```python
import functools

import jax
import jax.numpy as jnp
import numpy as np
from jax import lax
from jax.experimental import pallas as pl
from jax.experimental.pallas import tpu as pltpu
from jax.sharding import PartitionSpec as P

D = 1024
HEAD_DIM = 128
NSCALE = 7
SLOT = 136
PAD = 144
CHUNK = 48
SLABS = 4
ROWS = SLABS * PAD
COLS = 256
SIDES = (1, 2, 4, 6, 8, 12, 16)
TOK_IMG = 521
TOK_IN = 265
SIZE = {"x": 2, "y": 4, "z": 8}
ORDER = {
    ("out", 0): "zxy",
    ("out", 1): "yzx",
    ("v", 0): "xyz",
    ("v", 1): "yxz",
    ("q", 0): "zxy",
    ("k", 0): "xyz",
    ("q", 1): "xyz",
    ("k", 1): "yxz",
}
FINISH = (
    (("out", 1), 0),
    (("v", 0), 0),
    (("v", 1), 0),
    (("k", 0), 0),
    (("out", 0), 0),
    (("k", 1), 0),
    (("q", 1), 0),
    (("v", 1), 1),
    (("v", 0), 1),
    (("out", 0), 1),
    (("k", 0), 1),
    (("k", 1), 1),
    (("q", 0), 0),
    (("q", 1), 1),
    (("out", 0), 2),
    (("out", 1), 1),
    (("v", 1), 2),
    (("q", 0), 1),
    (("v", 0), 2),
    (("out", 1), 2),
    (("k", 0), 2),
    (("k", 1), 2),
    (("q", 0), 2),
    (("q", 1), 2),
)
PLACE = {"q": 0, "k": 1, "v": 2, "out": 3}
LOADED = (
    "stream",
    "residuals",
    "token_slot",
    "norm_gain",
    "embed_weight",
    "level_embed",
    "teacher_map",
    "out_grad",
)
MESH = pl.DeviceIdType.MESH
F32 = jnp.float32
BF16 = jnp.bfloat16


def line_matrix(source, target):
    places = np.arange(target)
    numerator = (2 * places + 1) * source - target
    low_index = numerator // (2 * target)
    fraction = (numerator - low_index * 2 * target) / (2.0 * target)
    fraction = np.where(numerator < 0, 0.0, fraction)
    low_index = np.maximum(low_index, 0)
    fraction = np.where(low_index >= source - 1, 0.0, fraction)
    low_index = np.minimum(low_index, source - 1)
    high_index = np.minimum(low_index + 1, source - 1)
    columns = np.arange(source)
    return (columns[None, :] == low_index[:, None]) * (1.0 - fraction[:, None]) + (
        columns[None, :] == high_index[:, None]
    ) * fraction[:, None]


def teacher_matrix():
    finest = SIDES[-1]
    starts = np.concatenate([[0], np.cumsum([s * s for s in SIDES])])
    whole = np.zeros((TOK_IMG, TOK_IN))
    for k in range(NSCALE - 1):
        down = line_matrix(finest, SIDES[k + 1])
        for j in range(k + 1):
            one = down @ line_matrix(SIDES[j], finest)
            whole[starts[k + 1] : starts[k + 2], starts[j] : starts[j + 1]] = np.kron(one, one)
    return whole.astype(np.float32)


def scale_of(shape, dim):
    token = lax.broadcasted_iota(jnp.int32, shape, dim)
    scale = jnp.full(shape, -NSCALE, jnp.int32)
    for start in np.cumsum([side * side for side in SIDES[:-1]]):
        scale = scale + jnp.where(token >= int(start), 1, 0)
    return scale


def dot(a, b, ca=1, cb=0, **kw):
    return lax.dot_general(
        a, b, (((ca,), (cb,)), ((), ())), preferred_element_type=F32, **kw
    )


def kernel(names, *refs):
    r = dict(zip(names, refs, strict=True))
    i, t = lax.axis_index("img"), lax.axis_index("tok")
    core, x_hi = lax.rem(t, 2), lax.div(t, 2)
    mine = {"x": lax.div(i, 32), "y": lax.rem(lax.div(i, 8), 4), "z": lax.rem(i, 8)}

    tok_of = [t, x_hi * 2 + (1 - core), (1 - x_hi) * 2 + core, (1 - x_hi) * 2 + (1 - core)]
    peer = [(i, n) for n in tok_of]

    def along(axis, d):
        at = dict(mine)
        at[axis] = lax.rem(mine[axis] + d, SIZE[axis])
        return ((at["x"] * 4 + at["y"]) * 8 + at["z"], t)

    friends = peer[1:] + [along(a, d) for a in "xyz" for d in range(1, SIZE[a])]
    barrier = pltpu.get_barrier_semaphore()
    for f in friends:
        pl.semaphore_signal(barrier, inc=1, device_id=f, device_id_type=MESH)

    sems, used = r["sems"], [0]

    def new_sem():
        used[0] += 1
        return sems.at[used[0] - 1]

    def remote(src, dst, device, send_sem, recv_sem):
        return pltpu.make_async_remote_copy(
            src_ref=src,
            dst_ref=dst,
            send_sem=send_sem,
            recv_sem=recv_sem,
            device_id=device,
            device_id_type=MESH,
        )

    def wait_bytes(ref, sem):
        pltpu.make_async_copy(ref, ref, sem).wait()

    small = {n: pltpu.make_async_copy(r[n], r["l_" + n], new_sem()) for n in LOADED}
    ow_sem, wq_sem = new_sem(), new_sem()
    loads = []
    for s in range(SLABS):
        at = pl.multiple_of(tok_of[s] * COLS, COLS)
        loads.append(
            pltpu.make_async_copy(r["out_weight"].at[:, pl.ds(at, COLS)], r["ow"].at[s], ow_sem)
        )
    for b in range(3):
        at = pl.multiple_of(b * D + t * COLS, COLS)
        loads.append(
            pltpu.make_async_copy(r["qkv_weight"].at[:, pl.ds(at, COLS)], r["wq"].at[b], wq_sem)
        )
    for load in list(small.values()) + loads:
        load.start()

    none = jnp.zeros((PAD - SLOT, D), F32)
    small["stream"].wait()
    r["sbuf"][0] = jnp.concatenate([r["l_stream"][0].astype(F32), none], 0).astype(BF16)
    small["residuals"].wait()
    r["res"][t] = r["l_residuals"][0]
    pl.semaphore_wait(barrier, len(friends))

    res_copies = [
        remote(r["res"].at[t], r["res"].at[t], peer[s], new_sem(), new_sem()) for s in (1, 2, 3)
    ]
    pieces = [pl.ds(CHUNK * c, CHUNK) for c in range(PAD // CHUNK)]

    def gather_copies(buf):
        sent, onward_sem = new_sem(), new_sem()
        cross = [remote(buf.at[0, p], buf.at[2, p], peer[2], new_sem(), new_sem()) for p in pieces]
        near = remote(buf.at[0], buf.at[1], peer[1], sent, new_sem())
        onward = [remote(buf.at[2, p], buf.at[3, p], peer[1], sent, onward_sem) for p in pieces]
        return cross, near, onward, sent, onward_sem

    s_cross, s_near, s_onward, s_sent, s_onward_sem = gather_copies(r["sbuf"])
    u_cross, u_near, u_onward, u_sent, u_onward_sem = gather_copies(r["ubuf"])
    for c in res_copies + s_cross + [s_near]:
        c.start()
    for n in LOADED[2:]:
        small[n].wait()
    r["ubuf"][0] = jnp.concatenate([r["l_out_grad"][0].astype(F32), none], 0).astype(BF16)

    row = lax.broadcasted_iota(jnp.int32, (ROWS, 1), 0)
    slot = jnp.full((ROWS, 1), -1, jnp.int32)
    for s in range(SLABS):
        inside = (row >= s * PAD) & (row < s * PAD + SLOT)
        slot = jnp.where(inside, row + (tok_of[s] * SLOT - s * PAD), slot)
    pick = jnp.where(slot == r["l_token_slot"][...], 1.0, 0.0).astype(BF16)
    lane = lax.broadcasted_iota(jnp.int32, (TOK_IMG, 8), 1)
    scale = scale_of((TOK_IMG, 8), 0)
    table = jnp.where(lane == scale + NSCALE, 1, 0) + jnp.where(lane == 7, scale, 0)
    levels = dot(pick, table.astype(F32).astype(BF16))
    sc_col = levels[:, 7:8]
    r["sc_col"][...] = sc_col
    r["sc_row"][...] = dot(
        scale_of((8, TOK_IMG), 1).astype(F32).astype(BF16), pick, 1, 1
    )
    for c in res_copies:
        c.wait_recv()
    teacher = dot(
        r["l_teacher_map"][...],
        r["res"][...].reshape(32, TOK_IN),
        1,
        1,
        precision=lax.Precision.HIGHEST,
    ).astype(BF16)
    r["chan"][...] = dot(pick, teacher).astype(BF16)
    r["lev"][...] = levels[:, :7].astype(BF16)

    def enter(s):
        at = pl.ds(s * PAD, PAD)
        base = dot(r["chan"][at, :], r["l_embed_weight"][...]) + dot(
            r["lev"][at, :], r["l_level_embed"][...]
        )
        block_in = (base + r["sbuf"][s].astype(F32)).astype(BF16)
        if s == 0:
            r["block_in"][...] = block_in
        x = block_in.astype(F32)
        scale = lax.rsqrt(jnp.mean(x * x, axis=-1, keepdims=True) + 1e-6)
        r["normed"][at, :] = (x * scale * r["l_norm_gain"][...]).astype(BF16)

    def project(first):
        at = pl.ds(first * PAD, 2 * PAD)
        for b in range(3):
            r["qkv"][b, at, :] = dot(r["normed"][at, :], r["wq"][b]).astype(BF16)

    enter(0)
    s_near.wait_recv()
    enter(1)
    wait_bytes(r["ow"], ow_sem)
    wait_bytes(r["wq"], wq_sem)
    project(0)
    for c in range(len(pieces)):
        s_cross[c].wait_send()
        u_cross[c].start()
    for c in range(len(pieces)):
        s_cross[c].wait_recv()
        s_onward[c].start()
    u_near.start()
    enter(2)
    wait_bytes(r["sbuf"].at[3], s_onward_sem)
    enter(3)
    project(2)

    factor = HEAD_DIM ** (-0.5)
    heads = [slice(h * HEAD_DIM, (h + 1) * HEAD_DIM) for h in range(2)]
    for h in range(2):
        k, v = r["qkv"][1, :, heads[h]], r["qkv"][2, :, heads[h]]
        for s in range(SLABS):
            at = pl.ds(s * PAD, PAD)
            scores = dot(r["qkv"][0, at, heads[h]], k, 1, 1)
            allowed = r["sc_row"][0:1, :] <= r["sc_col"][at, :]
            scores = jnp.where(allowed, scores, -jnp.inf)
            top = jnp.max(scores, axis=-1, keepdims=True)
            expd = jnp.exp2((scores - top) * (factor * np.log2(np.e)))
            total = jnp.sum(expd, axis=-1, keepdims=True)
            probs = (expd * (1.0 / total)).astype(BF16)
            r["probs"][h, at, :] = probs
            r["att"][s, :, heads[h]] = dot(probs, v).astype(BF16)

    for c in range(len(pieces)):
        u_cross[c].wait_recv()
        u_onward[c].start()
    a_sent, a_come = new_sem(), new_sem()
    for s in (1, 2, 3):
        remote(r["att"].at[s], r["attin"].at[s - 1], peer[s], a_sent, a_come).start()
    u_near.wait_recv()
    wait_bytes(r["ubuf"].at[3], u_onward_sem)
    for s in range(SLABS):
        at = pl.ds(s * PAD, PAD)
        up = jnp.where(r["sc_col"][at, :] < 0.0, r["ubuf"][s].astype(F32), 0.0)
        r["up"][at, :] = up.astype(BF16)

    piece_sent, arrival = {}, {}

    def tiles(name, stage):
        sizes = [SIZE[a] for a in ORDER[name]]
        share = (64, 32, 16, 8, 4, 2, 1)[sum(n.bit_length() - 1 for n in sizes[: stage + 1])]
        first = 64 - share * sizes[stage]
        return sizes[stage], share, first

    def first_stage(names, g):
        for n, name in enumerate(names):
            order, gf, gb = ORDER[name], r["gf", name], r["gb", name]
            _, n2, n3 = (SIZE[a] for a in order)
            step = {order[0]: n2 * n3, order[1]: n3, order[2]: 1}
            for x in range(2):
                for y in range(4):
                    rows = slice(x * 512 + y * 128, x * 512 + (y + 1) * 128)
                    part = g[rows, heads[n]].reshape(8, 16, HEAD_DIM)
                    at = x * step["x"] + y * step["y"]
                    if step["z"] == 1:
                        gf[at : at + 8] = part
                        gb[at : at + 8] = part.astype(BF16)
                    else:
                        for z in range(8):
                            gf[at + z * step["z"]] = part[z]
                            gb[at + z * step["z"]] = part[z].astype(BF16)
            piece_sent[name] = new_sem()
            start(name, 0, gb)

    def start(name, stage, src):
        axis = ORDER[name][stage]
        n, share, first = tiles(name, stage)
        arrival[name, stage] = new_sem()
        for d in range(1, n):
            remote(
                src.at[pl.ds(lax.rem(mine[axis] + d, n) * share, share)],
                r["in", name].at[pl.ds(first + (d - 1) * share, share)],
                along(axis, d),
                piece_sent[name],
                arrival[name, stage],
            ).start()

    def finish(name, stage):
        axis = ORDER[name][stage]
        n, share, first = tiles(name, stage)
        come = r["in", name]
        wait_bytes(come.at[pl.ds(first, (n - 1) * share)], arrival[name, stage])
        own = r["gf", name] if stage == 0 else r["sf", stage - 1, name]
        total = own[pl.ds(mine[axis] * share, share)]
        for d in range(1, n):
            total = total + come[pl.ds(first + (d - 1) * share, share)].astype(F32)
        if stage < 2:
            r["sf", stage, name][...] = total
            r["sb", stage, name][...] = total.astype(BF16)
            start(name, stage + 1, r["sb", stage, name])
        else:
            r["weight_grad"][PLACE[name[0]], :, heads[name[1]]] = total[0]

    att = jnp.concatenate([r["att"][s] for s in range(SLABS)], 0)
    first_stage((("out", 0), ("out", 1)), dot(r["up"][...], att, 0, 0))
    r["normed_t"][...] = r["normed"][...].T
    r["ag"][...] = dot(r["up"][...], r["ow"][0]).astype(BF16)
    for h in range(2):
        r["dv"][:, heads[h]] = dot(r["probs"][h], r["ag"][:, heads[h]], 0, 0).astype(BF16)
    first_stage((("v", 0), ("v", 1)), dot(r["normed_t"][...], r["dv"][...]))
    for h in range(2):
        k, v = r["qkv"][1, :, heads[h]], r["qkv"][2, :, heads[h]]
        for s in range(SLABS):
            at = pl.ds(s * PAD, PAD)
            dprobs = dot(r["ag"][at, heads[h]], v, 1, 1)
            probs = r["probs"][h, at, :].astype(F32)
            delta = jnp.sum(probs * dprobs, axis=-1, keepdims=True)
            ds = (probs * (dprobs - delta) * factor).astype(BF16)
            r["ds"][h, at, :] = ds
            r["dqk"][at, heads[0]] = dot(ds, k).astype(BF16)
        r["dqk"][:, heads[1]] = dot(r["ds"][h], r["qkv"][0, :, heads[h]], 0, 0).astype(BF16)
        first_stage((("q", h), ("k", h)), dot(r["normed_t"][...], r["dqk"][...]))

    wait_bytes(r["attin"], a_come)
    mixed = r["block_in"][...].astype(F32) + dot(r["att"][0], r["ow"][0], 1, 1)
    for s in (1, 2, 3):
        mixed = mixed + dot(r["attin"][s - 1], r["ow"][s], 1, 1)
    mixed = jnp.where(r["sc_col"][pl.ds(0, PAD), :] < 0.0, mixed, 0.0)
    r["done"][0] = mixed[:SLOT].astype(BF16)
    block_write = pltpu.make_async_copy(r["done"], r["block_out"], new_sem())
    block_write.start()

    for name, stage in FINISH:
        finish(name, stage)
    block_write.wait()
    for c in res_copies:
        c.wait_send()
    for c in u_cross:
        c.wait_send()
    wait_bytes(r["sbuf"].at[pl.ds(1, 2)], s_sent)
    wait_bytes(r["ubuf"].at[pl.ds(1, 2)], u_sent)
    wait_bytes(r["attin"], a_sent)
    for name in ORDER:
        wait_bytes(r["in", name], piece_sent[name])


def scratch():
    out = {
        "sems": pltpu.SemaphoreType.DMA((len(LOADED) + 2 + 6 + 18 + 2 + 33,)),
        "ow": pltpu.VMEM((SLABS, D, COLS), BF16),
        "wq": pltpu.VMEM((3, D, COLS), BF16),
        "res": pltpu.VMEM((4, 8, TOK_IN), F32),
        "sbuf": pltpu.VMEM((SLABS, PAD, D), BF16),
        "ubuf": pltpu.VMEM((SLABS, PAD, D), BF16),
        "sc_col": pltpu.VMEM((ROWS, 1), F32),
        "sc_row": pltpu.VMEM((8, ROWS), F32),
        "chan": pltpu.VMEM((ROWS, 32), BF16),
        "lev": pltpu.VMEM((ROWS, 7), BF16),
        "block_in": pltpu.VMEM((PAD, D), BF16),
        "normed": pltpu.VMEM((ROWS, D), BF16),
        "up": pltpu.VMEM((ROWS, D), BF16),
        "qkv": pltpu.VMEM((3, ROWS, COLS), BF16),
        "probs": pltpu.VMEM((2, ROWS, ROWS), BF16),
        "ds": pltpu.VMEM((2, ROWS, ROWS), BF16),
        "att": pltpu.VMEM((SLABS, PAD, COLS), BF16),
        "attin": pltpu.VMEM((SLABS - 1, PAD, COLS), BF16),
        "ag": pltpu.VMEM((ROWS, COLS), BF16),
        "dv": pltpu.VMEM((ROWS, COLS), BF16),
        "dqk": pltpu.VMEM((ROWS, COLS), BF16),
        "normed_t": pltpu.VMEM((D, ROWS), BF16),
        "l_stream": pltpu.VMEM((1, SLOT, D), BF16),
        "l_out_grad": pltpu.VMEM((1, SLOT, D), BF16),
        "done": pltpu.VMEM((1, SLOT, D), BF16),
        "l_residuals": pltpu.VMEM((1, 8, TOK_IN), F32),
        "l_token_slot": pltpu.VMEM((1, TOK_IMG), jnp.int32),
        "l_norm_gain": pltpu.VMEM((1, D), F32),
        "l_level_embed": pltpu.VMEM((NSCALE, D), BF16),
        "l_embed_weight": pltpu.VMEM((32, D), BF16),
        "l_teacher_map": pltpu.VMEM((TOK_IMG, TOK_IN), F32),
    }
    for name, order in ORDER.items():
        _, n2, n3 = (SIZE[a] for a in order)
        tail = (16, HEAD_DIM)
        out["gf", name] = pltpu.VMEM((64,) + tail, F32)
        out["gb", name] = pltpu.VMEM((64,) + tail, BF16)
        out["in", name] = pltpu.VMEM((63,) + tail, BF16)
        for stage, share in ((0, n2 * n3), (1, n3)):
            out["sf", stage, name] = pltpu.VMEM((share,) + tail, F32)
            out["sb", stage, name] = pltpu.VMEM((share,) + tail, BF16)
    return out


def hand_over(block_in, weight_in, block_out, qkv_out, out_out):
    block_out[...] = block_in[...]
    qkv_out[...] = weight_in[:3]
    out_out[...] = weight_in[3]


INPUTS = (
    "residuals",
    "stream",
    "token_slot",
    "level_embed",
    "embed_weight",
    "norm_gain",
    "qkv_weight",
    "out_weight",
    "out_grad",
    "teacher_map",
)
OUTPUTS = ("block_out", "weight_grad")


def per_device(*args):
    ins = dict(zip(INPUTS, args))
    ins["norm_gain"] = ins["norm_gain"].reshape(1, D)
    ins["teacher_map"] = jnp.asarray(teacher_matrix())
    buffers = scratch()
    vmem = pl.BlockSpec(memory_space=pltpu.VMEM)
    far = pl.BlockSpec(memory_space=pl.ANY)
    block_shape = jax.ShapeDtypeStruct((1, SLOT, D), BF16)
    block_out, weight_grad = pl.pallas_call(
        functools.partial(kernel, INPUTS + OUTPUTS + tuple(buffers)),
        out_shape=(block_shape, jax.ShapeDtypeStruct((4, 16, COLS), F32)),
        in_specs=[far] * len(INPUTS),
        out_specs=(far, vmem),
        scratch_shapes=list(buffers.values()),
        compiler_params=pltpu.CompilerParams(
            collective_id=0, has_side_effects=True, vmem_limit_bytes=56 << 20
        ),
    )(*[ins[n] for n in INPUTS])
    block_out, qkv_grad, out_grad = pl.pallas_call(
        hand_over,
        out_shape=(
            block_shape,
            jax.ShapeDtypeStruct((3, 16, COLS), F32),
            jax.ShapeDtypeStruct((16, COLS), F32),
        ),
        in_specs=[vmem] * 2,
        out_specs=(vmem,) * 3,
    )(block_out, weight_grad)
    return block_out, qkv_grad.transpose(1, 0, 2), out_grad


def solution(mesh):
    in_specs = (
        P("img", "tok", None),
        P("img", "tok", None),
        P("img", None),
        P(),
        P(),
        P(),
        P(),
        P(),
        P("img", "tok", None),
    )
    out_specs = (P("img", "tok", None), P("img", None, "tok"), P("img", "tok"))
    return jax.shard_map(
        per_device, mesh=mesh, in_specs=in_specs, out_specs=out_specs, check_vma=False
    )
```

```python
import functools

import jax
import jax.numpy as jnp
import numpy as np
from jax import lax
from jax.experimental import pallas as pl
from jax.experimental.pallas import tpu as pltpu
from jax.sharding import PartitionSpec as P

D = 1024
HEAD_DIM = 128
NSCALE = 7
SLOT = 136
PAD = 144
CHUNK = 48
SLABS = 4
ROWS = SLABS * PAD
COLS = 256
SIDES = (1, 2, 4, 6, 8, 12, 16)
TOK_IMG = 521
TOK_IN = 265
SIZE = {"x": 2, "y": 4, "z": 8}
ORDER = {
    ("out", 0): "zxy",
    ("out", 1): "yzx",
    ("v", 0): "xyz",
    ("v", 1): "yxz",
    ("q", 0): "zxy",
    ("k", 0): "xyz",
    ("q", 1): "xyz",
    ("k", 1): "yxz",
}
FINISH = (
    (("out", 1), 0),
    (("v", 0), 0),
    (("v", 1), 0),
    (("k", 0), 0),
    (("out", 0), 0),
    (("k", 1), 0),
    (("q", 1), 0),
    (("v", 1), 1),
    (("v", 0), 1),
    (("out", 0), 1),
    (("k", 0), 1),
    (("k", 1), 1),
    (("q", 0), 0),
    (("q", 1), 1),
    (("out", 0), 2),
    (("out", 1), 1),
    (("v", 1), 2),
    (("q", 0), 1),
    (("v", 0), 2),
    (("out", 1), 2),
    (("k", 0), 2),
    (("k", 1), 2),
    (("q", 0), 2),
    (("q", 1), 2),
)
PLACE = {"q": 0, "k": 1, "v": 2, "out": 3}
LOADED = (
    "stream",
    "residuals",
    "token_slot",
    "norm_gain",
    "embed_weight",
    "level_embed",
    "teacher_map",
    "out_grad",
)
MESH = pl.DeviceIdType.MESH
F32 = jnp.float32
BF16 = jnp.bfloat16


def line_matrix(source, target):
    places = np.arange(target)
    numerator = (2 * places + 1) * source - target
    low_index = numerator // (2 * target)
    fraction = (numerator - low_index * 2 * target) / (2.0 * target)
    fraction = np.where(numerator < 0, 0.0, fraction)
    low_index = np.maximum(low_index, 0)
    fraction = np.where(low_index >= source - 1, 0.0, fraction)
    low_index = np.minimum(low_index, source - 1)
    high_index = np.minimum(low_index + 1, source - 1)
    columns = np.arange(source)
    return (columns[None, :] == low_index[:, None]) * (1.0 - fraction[:, None]) + (
        columns[None, :] == high_index[:, None]
    ) * fraction[:, None]


def teacher_matrix():
    finest = SIDES[-1]
    starts = np.concatenate([[0], np.cumsum([s * s for s in SIDES])])
    whole = np.zeros((TOK_IMG, TOK_IN))
    for k in range(NSCALE - 1):
        down = line_matrix(finest, SIDES[k + 1])
        for j in range(k + 1):
            one = down @ line_matrix(SIDES[j], finest)
            whole[starts[k + 1] : starts[k + 2], starts[j] : starts[j + 1]] = np.kron(one, one)
    return whole.astype(np.float32)


def scale_of(shape, dim):
    token = lax.broadcasted_iota(jnp.int32, shape, dim)
    scale = jnp.full(shape, -NSCALE, jnp.int32)
    for start in np.cumsum([side * side for side in SIDES[:-1]]):
        scale = scale + jnp.where(token >= int(start), 1, 0)
    return scale


def dot(a, b, ca=1, cb=0, **kw):
    return lax.dot_general(
        a, b, (((ca,), (cb,)), ((), ())), preferred_element_type=F32, **kw
    )


def kernel(names, *refs):
    r = dict(zip(names, refs, strict=True))
    i, t = lax.axis_index("img"), lax.axis_index("tok")
    core, x_hi = lax.rem(t, 2), lax.div(t, 2)
    mine = {"x": lax.div(i, 32), "y": lax.rem(lax.div(i, 8), 4), "z": lax.rem(i, 8)}

    tok_of = [t, x_hi * 2 + (1 - core), (1 - x_hi) * 2 + core, (1 - x_hi) * 2 + (1 - core)]
    peer = [(i, n) for n in tok_of]

    def along(axis, d):
        at = dict(mine)
        at[axis] = lax.rem(mine[axis] + d, SIZE[axis])
        return ((at["x"] * 4 + at["y"]) * 8 + at["z"], t)

    friends = peer[1:] + [along(a, d) for a in "xyz" for d in range(1, SIZE[a])]
    barrier = pltpu.get_barrier_semaphore()
    for f in friends:
        pl.semaphore_signal(barrier, inc=1, device_id=f, device_id_type=MESH)

    sems, used = r["sems"], [0]

    def new_sem():
        used[0] += 1
        return sems.at[used[0] - 1]

    def remote(src, dst, device, send_sem, recv_sem):
        return pltpu.make_async_remote_copy(
            src_ref=src,
            dst_ref=dst,
            send_sem=send_sem,
            recv_sem=recv_sem,
            device_id=device,
            device_id_type=MESH,
        )

    def wait_bytes(ref, sem):
        pltpu.make_async_copy(ref, ref, sem).wait()

    small = {n: pltpu.make_async_copy(r[n], r["l_" + n], new_sem()) for n in LOADED}
    ow_sem, wq_sem = new_sem(), new_sem()
    loads = []
    for s in range(SLABS):
        at = pl.multiple_of(tok_of[s] * COLS, COLS)
        loads.append(
            pltpu.make_async_copy(r["out_weight"].at[:, pl.ds(at, COLS)], r["ow"].at[s], ow_sem)
        )
    for b in range(3):
        at = pl.multiple_of(b * D + t * COLS, COLS)
        loads.append(
            pltpu.make_async_copy(r["qkv_weight"].at[:, pl.ds(at, COLS)], r["wq"].at[b], wq_sem)
        )
    for load in list(small.values()) + loads:
        load.start()

    none = jnp.zeros((PAD - SLOT, D), F32)
    small["stream"].wait()
    r["sbuf"][0] = jnp.concatenate([r["l_stream"][0].astype(F32), none], 0).astype(BF16)
    small["residuals"].wait()
    r["res"][t] = r["l_residuals"][0]
    pl.semaphore_wait(barrier, len(friends))

    res_copies = [
        remote(r["res"].at[t], r["res"].at[t], peer[s], new_sem(), new_sem()) for s in (1, 2, 3)
    ]
    pieces = [pl.ds(CHUNK * c, CHUNK) for c in range(PAD // CHUNK)]

    def gather_copies(buf):
        sent, onward_sem = new_sem(), new_sem()
        cross = [remote(buf.at[0, p], buf.at[2, p], peer[2], new_sem(), new_sem()) for p in pieces]
        near = remote(buf.at[0], buf.at[1], peer[1], sent, new_sem())
        onward = [remote(buf.at[2, p], buf.at[3, p], peer[1], sent, onward_sem) for p in pieces]
        return cross, near, onward, sent, onward_sem

    s_cross, s_near, s_onward, s_sent, s_onward_sem = gather_copies(r["sbuf"])
    u_cross, u_near, u_onward, u_sent, u_onward_sem = gather_copies(r["ubuf"])
    for c in res_copies + s_cross + [s_near]:
        c.start()
    for n in LOADED[2:]:
        small[n].wait()
    r["ubuf"][0] = jnp.concatenate([r["l_out_grad"][0].astype(F32), none], 0).astype(BF16)

    row = lax.broadcasted_iota(jnp.int32, (ROWS, 1), 0)
    slot = jnp.full((ROWS, 1), -1, jnp.int32)
    for s in range(SLABS):
        inside = (row >= s * PAD) & (row < s * PAD + SLOT)
        slot = jnp.where(inside, row + (tok_of[s] * SLOT - s * PAD), slot)
    pick = jnp.where(slot == r["l_token_slot"][...], 1.0, 0.0).astype(BF16)
    lane = lax.broadcasted_iota(jnp.int32, (TOK_IMG, 8), 1)
    scale = scale_of((TOK_IMG, 8), 0)
    table = jnp.where(lane == scale + NSCALE, 1, 0) + jnp.where(lane == 7, scale, 0)
    levels = dot(pick, table.astype(F32).astype(BF16))
    sc_col = levels[:, 7:8]
    r["sc_col"][...] = sc_col
    r["sc_row"][...] = dot(
        scale_of((8, TOK_IMG), 1).astype(F32).astype(BF16), pick, 1, 1
    )
    for c in res_copies:
        c.wait_recv()
    teacher = dot(
        r["l_teacher_map"][...],
        r["res"][...].reshape(32, TOK_IN),
        1,
        1,
        precision=lax.Precision.HIGHEST,
    ).astype(BF16)
    r["chan"][...] = dot(pick, teacher).astype(BF16)
    r["lev"][...] = levels[:, :7].astype(BF16)

    def enter(s):
        at = pl.ds(s * PAD, PAD)
        base = dot(r["chan"][at, :], r["l_embed_weight"][...]) + dot(
            r["lev"][at, :], r["l_level_embed"][...]
        )
        block_in = (base + r["sbuf"][s].astype(F32)).astype(BF16)
        if s == 0:
            r["block_in"][...] = block_in
        x = block_in.astype(F32)
        scale = lax.rsqrt(jnp.mean(x * x, axis=-1, keepdims=True) + 1e-6)
        r["normed"][at, :] = (x * scale * r["l_norm_gain"][...]).astype(BF16)

    def project(first):
        at = pl.ds(first * PAD, 2 * PAD)
        for b in range(3):
            r["qkv"][b, at, :] = dot(r["normed"][at, :], r["wq"][b]).astype(BF16)

    enter(0)
    s_near.wait_recv()
    enter(1)
    wait_bytes(r["ow"], ow_sem)
    wait_bytes(r["wq"], wq_sem)
    project(0)
    for c in range(len(pieces)):
        s_cross[c].wait_send()
        u_cross[c].start()
    for c in range(len(pieces)):
        s_cross[c].wait_recv()
        s_onward[c].start()
    u_near.start()
    enter(2)
    wait_bytes(r["sbuf"].at[3], s_onward_sem)
    enter(3)
    project(2)

    factor = HEAD_DIM ** (-0.5)
    heads = [slice(h * HEAD_DIM, (h + 1) * HEAD_DIM) for h in range(2)]
    for h in range(2):
        k, v = r["qkv"][1, :, heads[h]], r["qkv"][2, :, heads[h]]
        for s in range(SLABS):
            at = pl.ds(s * PAD, PAD)
            scores = dot(r["qkv"][0, at, heads[h]], k, 1, 1)
            allowed = r["sc_row"][0:1, :] <= r["sc_col"][at, :]
            scores = jnp.where(allowed, scores, -jnp.inf)
            top = jnp.max(scores, axis=-1, keepdims=True)
            expd = jnp.exp2((scores - top) * (factor * np.log2(np.e)))
            total = jnp.sum(expd, axis=-1, keepdims=True)
            probs = (expd * (1.0 / total)).astype(BF16)
            r["probs"][h, at, :] = probs
            r["att"][s, :, heads[h]] = dot(probs, v).astype(BF16)
            if h == 1 and s >= 1:
                u_cross[s - 1].wait_recv()
                u_onward[s - 1].start()

    a_sent, a_come = new_sem(), new_sem()
    for s in (1, 2, 3):
        remote(r["att"].at[s], r["attin"].at[s - 1], peer[s], a_sent, a_come).start()
    u_near.wait_recv()
    for s in range(SLABS):
        if s == 3:
            r["ag"][pl.ds(0, 3 * PAD), :] = dot(
                r["up"][pl.ds(0, 3 * PAD), :], r["ow"][0]
            ).astype(BF16)
            wait_bytes(r["ubuf"].at[3], u_onward_sem)
        at = pl.ds(s * PAD, PAD)
        up = jnp.where(r["sc_col"][at, :] < 0.0, r["ubuf"][s].astype(F32), 0.0)
        r["up"][at, :] = up.astype(BF16)

    piece_sent, arrival = {}, {}

    def tiles(name, stage):
        sizes = [SIZE[a] for a in ORDER[name]]
        share = (64, 32, 16, 8, 4, 2, 1)[sum(n.bit_length() - 1 for n in sizes[: stage + 1])]
        first = 64 - share * sizes[stage]
        return sizes[stage], share, first

    def first_stage(names, g):
        for n, name in enumerate(names):
            order, gf, gb = ORDER[name], r["gf", name], r["gb", name]
            _, n2, n3 = (SIZE[a] for a in order)
            step = {order[0]: n2 * n3, order[1]: n3, order[2]: 1}
            for x in range(2):
                for y in range(4):
                    rows = slice(x * 512 + y * 128, x * 512 + (y + 1) * 128)
                    part = g[rows, heads[n]].reshape(8, 16, HEAD_DIM)
                    at = x * step["x"] + y * step["y"]
                    if step["z"] == 1:
                        gf[at : at + 8] = part
                        gb[at : at + 8] = part.astype(BF16)
                    else:
                        for z in range(8):
                            gf[at + z * step["z"]] = part[z]
                            gb[at + z * step["z"]] = part[z].astype(BF16)
            piece_sent[name] = new_sem()
            start(name, 0, gb)

    def start(name, stage, src):
        axis = ORDER[name][stage]
        n, share, first = tiles(name, stage)
        arrival[name, stage] = new_sem()
        for d in range(1, n):
            remote(
                src.at[pl.ds(lax.rem(mine[axis] + d, n) * share, share)],
                r["in", name].at[pl.ds(first + (d - 1) * share, share)],
                along(axis, d),
                piece_sent[name],
                arrival[name, stage],
            ).start()

    def finish(name, stage):
        axis = ORDER[name][stage]
        n, share, first = tiles(name, stage)
        come = r["in", name]
        wait_bytes(come.at[pl.ds(first, (n - 1) * share)], arrival[name, stage])
        own = r["gf", name] if stage == 0 else r["sf", stage - 1, name]
        total = own[pl.ds(mine[axis] * share, share)]
        for d in range(1, n):
            total = total + come[pl.ds(first + (d - 1) * share, share)].astype(F32)
        if stage < 2:
            r["sf", stage, name][...] = total
            r["sb", stage, name][...] = total.astype(BF16)
            start(name, stage + 1, r["sb", stage, name])
        else:
            r["weight_grad"][PLACE[name[0]], :, heads[name[1]]] = total[0]

    att = jnp.concatenate([r["att"][s] for s in range(SLABS)], 0)
    first_stage((("out", 0), ("out", 1)), dot(r["up"][...], att, 0, 0))
    r["normed_t"][...] = r["normed"][...].T
    last = pl.ds(3 * PAD, PAD)
    r["ag"][last, :] = dot(r["up"][last, :], r["ow"][0]).astype(BF16)
    for h in range(2):
        r["dv"][:, heads[h]] = dot(r["probs"][h], r["ag"][:, heads[h]], 0, 0).astype(BF16)
    first_stage((("v", 0), ("v", 1)), dot(r["normed_t"][...], r["dv"][...]))
    for h in range(2):
        k, v = r["qkv"][1, :, heads[h]], r["qkv"][2, :, heads[h]]
        for s in range(SLABS):
            at = pl.ds(s * PAD, PAD)
            dprobs = dot(r["ag"][at, heads[h]], v, 1, 1)
            probs = r["probs"][h, at, :].astype(F32)
            delta = jnp.sum(probs * dprobs, axis=-1, keepdims=True)
            ds = (probs * (dprobs - delta) * factor).astype(BF16)
            r["ds"][h, at, :] = ds
            r["dqk"][at, heads[0]] = dot(ds, k).astype(BF16)
        r["dqk"][:, heads[1]] = dot(r["ds"][h], r["qkv"][0, :, heads[h]], 0, 0).astype(BF16)
        first_stage((("q", h), ("k", h)), dot(r["normed_t"][...], r["dqk"][...]))

    wait_bytes(r["attin"], a_come)
    mixed = r["block_in"][...].astype(F32) + dot(r["att"][0], r["ow"][0], 1, 1)
    for s in (1, 2, 3):
        mixed = mixed + dot(r["attin"][s - 1], r["ow"][s], 1, 1)
    mixed = jnp.where(r["sc_col"][pl.ds(0, PAD), :] < 0.0, mixed, 0.0)
    r["done"][0] = mixed[:SLOT].astype(BF16)
    block_write = pltpu.make_async_copy(r["done"], r["block_out"], new_sem())
    block_write.start()

    for name, stage in FINISH:
        finish(name, stage)
    block_write.wait()
    for c in res_copies:
        c.wait_send()
    for c in u_cross:
        c.wait_send()
    wait_bytes(r["sbuf"].at[pl.ds(1, 2)], s_sent)
    wait_bytes(r["ubuf"].at[pl.ds(1, 2)], u_sent)
    wait_bytes(r["attin"], a_sent)
    for name in ORDER:
        wait_bytes(r["in", name], piece_sent[name])


def scratch():
    out = {
        "sems": pltpu.SemaphoreType.DMA((len(LOADED) + 2 + 6 + 18 + 2 + 33,)),
        "ow": pltpu.VMEM((SLABS, D, COLS), BF16),
        "wq": pltpu.VMEM((3, D, COLS), BF16),
        "res": pltpu.VMEM((4, 8, TOK_IN), F32),
        "sbuf": pltpu.VMEM((SLABS, PAD, D), BF16),
        "ubuf": pltpu.VMEM((SLABS, PAD, D), BF16),
        "sc_col": pltpu.VMEM((ROWS, 1), F32),
        "sc_row": pltpu.VMEM((8, ROWS), F32),
        "chan": pltpu.VMEM((ROWS, 32), BF16),
        "lev": pltpu.VMEM((ROWS, 7), BF16),
        "block_in": pltpu.VMEM((PAD, D), BF16),
        "normed": pltpu.VMEM((ROWS, D), BF16),
        "up": pltpu.VMEM((ROWS, D), BF16),
        "qkv": pltpu.VMEM((3, ROWS, COLS), BF16),
        "probs": pltpu.VMEM((2, ROWS, ROWS), BF16),
        "ds": pltpu.VMEM((2, ROWS, ROWS), BF16),
        "att": pltpu.VMEM((SLABS, PAD, COLS), BF16),
        "attin": pltpu.VMEM((SLABS - 1, PAD, COLS), BF16),
        "ag": pltpu.VMEM((ROWS, COLS), BF16),
        "dv": pltpu.VMEM((ROWS, COLS), BF16),
        "dqk": pltpu.VMEM((ROWS, COLS), BF16),
        "normed_t": pltpu.VMEM((D, ROWS), BF16),
        "l_stream": pltpu.VMEM((1, SLOT, D), BF16),
        "l_out_grad": pltpu.VMEM((1, SLOT, D), BF16),
        "done": pltpu.VMEM((1, SLOT, D), BF16),
        "l_residuals": pltpu.VMEM((1, 8, TOK_IN), F32),
        "l_token_slot": pltpu.VMEM((1, TOK_IMG), jnp.int32),
        "l_norm_gain": pltpu.VMEM((1, D), F32),
        "l_level_embed": pltpu.VMEM((NSCALE, D), BF16),
        "l_embed_weight": pltpu.VMEM((32, D), BF16),
        "l_teacher_map": pltpu.VMEM((TOK_IMG, TOK_IN), F32),
    }
    for name, order in ORDER.items():
        _, n2, n3 = (SIZE[a] for a in order)
        tail = (16, HEAD_DIM)
        out["gf", name] = pltpu.VMEM((64,) + tail, F32)
        out["gb", name] = pltpu.VMEM((64,) + tail, BF16)
        out["in", name] = pltpu.VMEM((63,) + tail, BF16)
        for stage, share in ((0, n2 * n3), (1, n3)):
            out["sf", stage, name] = pltpu.VMEM((share,) + tail, F32)
            out["sb", stage, name] = pltpu.VMEM((share,) + tail, BF16)
    return out


def hand_over(block_in, weight_in, block_out, qkv_out, out_out):
    block_out[...] = block_in[...]
    qkv_out[...] = weight_in[:3]
    out_out[...] = weight_in[3]


INPUTS = (
    "residuals",
    "stream",
    "token_slot",
    "level_embed",
    "embed_weight",
    "norm_gain",
    "qkv_weight",
    "out_weight",
    "out_grad",
    "teacher_map",
)
OUTPUTS = ("block_out", "weight_grad")


def per_device(*args):
    ins = dict(zip(INPUTS, args))
    ins["norm_gain"] = ins["norm_gain"].reshape(1, D)
    ins["teacher_map"] = jnp.asarray(teacher_matrix())
    buffers = scratch()
    vmem = pl.BlockSpec(memory_space=pltpu.VMEM)
    far = pl.BlockSpec(memory_space=pl.ANY)
    block_shape = jax.ShapeDtypeStruct((1, SLOT, D), BF16)
    block_out, weight_grad = pl.pallas_call(
        functools.partial(kernel, INPUTS + OUTPUTS + tuple(buffers)),
        out_shape=(block_shape, jax.ShapeDtypeStruct((4, 16, COLS), F32)),
        in_specs=[far] * len(INPUTS),
        out_specs=(far, vmem),
        scratch_shapes=list(buffers.values()),
        compiler_params=pltpu.CompilerParams(
            collective_id=0, has_side_effects=True, vmem_limit_bytes=56 << 20
        ),
    )(*[ins[n] for n in INPUTS])
    block_out, qkv_grad, out_grad = pl.pallas_call(
        hand_over,
        out_shape=(
            block_shape,
            jax.ShapeDtypeStruct((3, 16, COLS), F32),
            jax.ShapeDtypeStruct((16, COLS), F32),
        ),
        in_specs=[vmem] * 2,
        out_specs=(vmem,) * 3,
    )(block_out, weight_grad)
    return block_out, qkv_grad.transpose(1, 0, 2), out_grad


def solution(mesh):
    in_specs = (
        P("img", "tok", None),
        P("img", "tok", None),
        P("img", None),
        P(),
        P(),
        P(),
        P(),
        P(),
        P("img", "tok", None),
    )
    out_specs = (P("img", "tok", None), P("img", None, "tok"), P("img", "tok"))
    return jax.shard_map(
        per_device, mesh=mesh, in_specs=in_specs, out_specs=out_specs, check_vma=False
    )
```

```python
import functools

import jax
import jax.numpy as jnp
import numpy as np
from jax import lax
from jax.experimental import pallas as pl
from jax.experimental.pallas import tpu as pltpu
from jax.sharding import PartitionSpec as P

D = 1024
HEAD_DIM = 128
NSCALE = 7
SLOT = 136
PAD = 144
CHUNK = 48
SLABS = 4
ROWS = SLABS * PAD
COLS = 256
SIDES = (1, 2, 4, 6, 8, 12, 16)
TOK_IMG = 521
TOK_IN = 265
SIZE = {"x": 2, "y": 4, "z": 8}
ORDER = {
    ("out", 0): "zxy",
    ("out", 1): "yzx",
    ("v", 0): "xyz",
    ("v", 1): "yxz",
    ("q", 0): "zxy",
    ("k", 0): "xyz",
    ("q", 1): "xyz",
    ("k", 1): "yxz",
}
FINISH = (
    (("out", 1), 0),
    (("v", 0), 0),
    (("v", 1), 0),
    (("k", 0), 0),
    (("out", 0), 0),
    (("k", 1), 0),
    (("q", 1), 0),
    (("v", 1), 1),
    (("v", 0), 1),
    (("out", 0), 1),
    (("k", 0), 1),
    (("k", 1), 1),
    (("q", 0), 0),
    (("q", 1), 1),
    (("out", 0), 2),
    (("out", 1), 1),
    (("v", 1), 2),
    (("q", 0), 1),
    (("v", 0), 2),
    (("out", 1), 2),
    (("k", 0), 2),
    (("k", 1), 2),
    (("q", 0), 2),
    (("q", 1), 2),
)
PLACE = {"q": 0, "k": 1, "v": 2, "out": 3}
LOADED = (
    "stream",
    "residuals",
    "token_slot",
    "norm_gain",
    "embed_weight",
    "level_embed",
    "teacher_map",
    "out_grad",
)
MESH = pl.DeviceIdType.MESH
F32 = jnp.float32
BF16 = jnp.bfloat16


def line_matrix(source, target):
    places = np.arange(target)
    numerator = (2 * places + 1) * source - target
    low_index = numerator // (2 * target)
    fraction = (numerator - low_index * 2 * target) / (2.0 * target)
    fraction = np.where(numerator < 0, 0.0, fraction)
    low_index = np.maximum(low_index, 0)
    fraction = np.where(low_index >= source - 1, 0.0, fraction)
    low_index = np.minimum(low_index, source - 1)
    high_index = np.minimum(low_index + 1, source - 1)
    columns = np.arange(source)
    return (columns[None, :] == low_index[:, None]) * (1.0 - fraction[:, None]) + (
        columns[None, :] == high_index[:, None]
    ) * fraction[:, None]


def teacher_matrix():
    finest = SIDES[-1]
    starts = np.concatenate([[0], np.cumsum([s * s for s in SIDES])])
    whole = np.zeros((TOK_IMG, TOK_IN))
    for k in range(NSCALE - 1):
        down = line_matrix(finest, SIDES[k + 1])
        for j in range(k + 1):
            one = down @ line_matrix(SIDES[j], finest)
            whole[starts[k + 1] : starts[k + 2], starts[j] : starts[j + 1]] = np.kron(one, one)
    return whole.astype(np.float32)


def scale_of(shape, dim):
    token = lax.broadcasted_iota(jnp.int32, shape, dim)
    scale = jnp.full(shape, -NSCALE, jnp.int32)
    for start in np.cumsum([side * side for side in SIDES[:-1]]):
        scale = scale + jnp.where(token >= int(start), 1, 0)
    return scale


def dot(a, b, ca=1, cb=0, **kw):
    return lax.dot_general(
        a, b, (((ca,), (cb,)), ((), ())), preferred_element_type=F32, **kw
    )


def kernel(names, *refs):
    r = dict(zip(names, refs, strict=True))
    i, t = lax.axis_index("img"), lax.axis_index("tok")
    core, x_hi = lax.rem(t, 2), lax.div(t, 2)
    mine = {"x": lax.div(i, 32), "y": lax.rem(lax.div(i, 8), 4), "z": lax.rem(i, 8)}

    tok_of = [t, x_hi * 2 + (1 - core), (1 - x_hi) * 2 + core, (1 - x_hi) * 2 + (1 - core)]
    peer = [(i, n) for n in tok_of]

    def along(axis, d):
        at = dict(mine)
        at[axis] = lax.rem(mine[axis] + d, SIZE[axis])
        return ((at["x"] * 4 + at["y"]) * 8 + at["z"], t)

    friends = peer[1:] + [along(a, d) for a in "xyz" for d in range(1, SIZE[a])]
    barrier = pltpu.get_barrier_semaphore()
    for f in friends:
        pl.semaphore_signal(barrier, inc=1, device_id=f, device_id_type=MESH)

    sems, used = r["sems"], [0]

    def new_sem():
        used[0] += 1
        return sems.at[used[0] - 1]

    def remote(src, dst, device, send_sem, recv_sem):
        return pltpu.make_async_remote_copy(
            src_ref=src,
            dst_ref=dst,
            send_sem=send_sem,
            recv_sem=recv_sem,
            device_id=device,
            device_id_type=MESH,
        )

    def wait_bytes(ref, sem):
        pltpu.make_async_copy(ref, ref, sem).wait()

    small = {n: pltpu.make_async_copy(r[n], r["l_" + n], new_sem()) for n in LOADED}
    ow_sem, wq_sem = new_sem(), new_sem()
    loads = []
    for s in range(SLABS):
        at = pl.multiple_of(tok_of[s] * COLS, COLS)
        loads.append(
            pltpu.make_async_copy(r["out_weight"].at[:, pl.ds(at, COLS)], r["ow"].at[s], ow_sem)
        )
    for b in range(3):
        at = pl.multiple_of(b * D + t * COLS, COLS)
        loads.append(
            pltpu.make_async_copy(r["qkv_weight"].at[:, pl.ds(at, COLS)], r["wq"].at[b], wq_sem)
        )
    for load in list(small.values()) + loads:
        load.start()

    none = jnp.zeros((PAD - SLOT, D), F32)
    small["stream"].wait()
    r["sbuf"][0] = jnp.concatenate([r["l_stream"][0].astype(F32), none], 0).astype(BF16)
    small["residuals"].wait()
    r["res"][t] = r["l_residuals"][0]
    pl.semaphore_wait(barrier, len(friends))

    res_copies = [
        remote(r["res"].at[t], r["res"].at[t], peer[s], new_sem(), new_sem()) for s in (1, 2, 3)
    ]
    pieces = [pl.ds(CHUNK * c, CHUNK) for c in range(PAD // CHUNK)]

    def gather_copies(buf):
        sent, onward_sem = new_sem(), new_sem()
        cross = [remote(buf.at[0, p], buf.at[2, p], peer[2], new_sem(), new_sem()) for p in pieces]
        near = remote(buf.at[0], buf.at[1], peer[1], sent, new_sem())
        onward = [remote(buf.at[2, p], buf.at[3, p], peer[1], sent, onward_sem) for p in pieces]
        return cross, near, onward, sent, onward_sem

    s_cross, s_near, s_onward, s_sent, s_onward_sem = gather_copies(r["sbuf"])
    u_cross, u_near, u_onward, u_sent, u_onward_sem = gather_copies(r["ubuf"])
    for c in res_copies + s_cross + [s_near]:
        c.start()
    for n in LOADED[2:]:
        small[n].wait()
    r["ubuf"][0] = jnp.concatenate([r["l_out_grad"][0].astype(F32), none], 0).astype(BF16)

    row = lax.broadcasted_iota(jnp.int32, (ROWS, 1), 0)
    slot = jnp.full((ROWS, 1), -1, jnp.int32)
    for s in range(SLABS):
        inside = (row >= s * PAD) & (row < s * PAD + SLOT)
        slot = jnp.where(inside, row + (tok_of[s] * SLOT - s * PAD), slot)
    pick = jnp.where(slot == r["l_token_slot"][...], 1.0, 0.0).astype(BF16)
    lane = lax.broadcasted_iota(jnp.int32, (TOK_IMG, 8), 1)
    scale = scale_of((TOK_IMG, 8), 0)
    table = jnp.where(lane == scale + NSCALE, 1, 0) + jnp.where(lane == 7, scale, 0)
    levels = dot(pick, table.astype(F32).astype(BF16))
    sc_col = levels[:, 7:8]
    r["sc_col"][...] = sc_col
    r["sc_row"][...] = dot(
        scale_of((8, TOK_IMG), 1).astype(F32).astype(BF16), pick, 1, 1
    )
    for c in res_copies:
        c.wait_recv()
    teacher = dot(
        r["l_teacher_map"][...],
        r["res"][...].reshape(32, TOK_IN),
        1,
        1,
        precision=lax.Precision.HIGHEST,
    ).astype(BF16)
    r["chan"][...] = dot(pick, teacher).astype(BF16)
    r["lev"][...] = levels[:, :7].astype(BF16)

    def enter(s):
        at = pl.ds(s * PAD, PAD)
        base = dot(r["chan"][at, :], r["l_embed_weight"][...]) + dot(
            r["lev"][at, :], r["l_level_embed"][...]
        )
        block_in = (base + r["sbuf"][s].astype(F32)).astype(BF16)
        if s == 0:
            r["block_in"][...] = block_in
        x = block_in.astype(F32)
        scale = lax.rsqrt(jnp.mean(x * x, axis=-1, keepdims=True) + 1e-6)
        r["normed"][at, :] = (x * scale * r["l_norm_gain"][...]).astype(BF16)

    def project(first, count):
        at = pl.ds(first * PAD, count * PAD)
        for b in range(3):
            r["qkv"][b, at, :] = dot(r["normed"][at, :], r["wq"][b]).astype(BF16)

    enter(0)
    s_near.wait_recv()
    enter(1)
    wait_bytes(r["ow"], ow_sem)
    wait_bytes(r["wq"], wq_sem)
    project(0, 2)
    for c in range(len(pieces)):
        s_cross[c].wait_send()
        u_cross[c].start()
    for c in range(len(pieces)):
        s_cross[c].wait_recv()
        s_onward[c].start()
    u_near.start()
    enter(2)
    project(2, 1)
    wait_bytes(r["sbuf"].at[3], s_onward_sem)
    enter(3)
    project(3, 1)

    factor = HEAD_DIM ** (-0.5)
    heads = [slice(h * HEAD_DIM, (h + 1) * HEAD_DIM) for h in range(2)]
    for h in range(2):
        k, v = r["qkv"][1, :, heads[h]], r["qkv"][2, :, heads[h]]
        for s in range(SLABS):
            at = pl.ds(s * PAD, PAD)
            scores = dot(r["qkv"][0, at, heads[h]], k, 1, 1)
            allowed = r["sc_row"][0:1, :] <= r["sc_col"][at, :]
            scores = jnp.where(allowed, scores, -jnp.inf)
            top = jnp.max(scores, axis=-1, keepdims=True)
            expd = jnp.exp2((scores - top) * (factor * np.log2(np.e)))
            total = jnp.sum(expd, axis=-1, keepdims=True)
            probs = (expd * (1.0 / total)).astype(BF16)
            r["probs"][h, at, :] = probs
            r["att"][s, :, heads[h]] = dot(probs, v).astype(BF16)
            if h == 1 and s >= 1:
                u_cross[s - 1].wait_recv()
                u_onward[s - 1].start()

    a_sent, a_come = new_sem(), new_sem()
    for s in (1, 2, 3):
        remote(r["att"].at[s], r["attin"].at[s - 1], peer[s], a_sent, a_come).start()
    u_near.wait_recv()
    for s in range(SLABS):
        if s == 3:
            r["ag"][pl.ds(0, 3 * PAD), :] = dot(
                r["up"][pl.ds(0, 3 * PAD), :], r["ow"][0]
            ).astype(BF16)
            wait_bytes(r["ubuf"].at[3], u_onward_sem)
        at = pl.ds(s * PAD, PAD)
        up = jnp.where(r["sc_col"][at, :] < 0.0, r["ubuf"][s].astype(F32), 0.0)
        r["up"][at, :] = up.astype(BF16)

    piece_sent, arrival = {}, {}

    def tiles(name, stage):
        sizes = [SIZE[a] for a in ORDER[name]]
        share = (64, 32, 16, 8, 4, 2, 1)[sum(n.bit_length() - 1 for n in sizes[: stage + 1])]
        first = 64 - share * sizes[stage]
        return sizes[stage], share, first

    def first_stage(names, g):
        for n, name in enumerate(names):
            order, gf, gb = ORDER[name], r["gf", name], r["gb", name]
            _, n2, n3 = (SIZE[a] for a in order)
            step = {order[0]: n2 * n3, order[1]: n3, order[2]: 1}
            for x in range(2):
                for y in range(4):
                    rows = slice(x * 512 + y * 128, x * 512 + (y + 1) * 128)
                    part = g[rows, heads[n]].reshape(8, 16, HEAD_DIM)
                    at = x * step["x"] + y * step["y"]
                    if step["z"] == 1:
                        gf[at : at + 8] = part
                        gb[at : at + 8] = part.astype(BF16)
                    else:
                        for z in range(8):
                            gf[at + z * step["z"]] = part[z]
                            gb[at + z * step["z"]] = part[z].astype(BF16)
            piece_sent[name] = new_sem()
            start(name, 0, gb)

    def start(name, stage, src):
        axis = ORDER[name][stage]
        n, share, first = tiles(name, stage)
        arrival[name, stage] = new_sem()
        for d in range(1, n):
            remote(
                src.at[pl.ds(lax.rem(mine[axis] + d, n) * share, share)],
                r["in", name].at[pl.ds(first + (d - 1) * share, share)],
                along(axis, d),
                piece_sent[name],
                arrival[name, stage],
            ).start()

    def finish(name, stage):
        axis = ORDER[name][stage]
        n, share, first = tiles(name, stage)
        come = r["in", name]
        wait_bytes(come.at[pl.ds(first, (n - 1) * share)], arrival[name, stage])
        own = r["gf", name] if stage == 0 else r["sf", stage - 1, name]
        total = own[pl.ds(mine[axis] * share, share)]
        for d in range(1, n):
            total = total + come[pl.ds(first + (d - 1) * share, share)].astype(F32)
        if stage < 2:
            r["sf", stage, name][...] = total
            r["sb", stage, name][...] = total.astype(BF16)
            start(name, stage + 1, r["sb", stage, name])
        else:
            r["weight_grad"][PLACE[name[0]], :, heads[name[1]]] = total[0]

    att = jnp.concatenate([r["att"][s] for s in range(SLABS)], 0)
    first_stage((("out", 0), ("out", 1)), dot(r["up"][...], att, 0, 0))
    r["normed_t"][...] = r["normed"][...].T
    last = pl.ds(3 * PAD, PAD)
    r["ag"][last, :] = dot(r["up"][last, :], r["ow"][0]).astype(BF16)
    for h in range(2):
        r["dv"][:, heads[h]] = dot(r["probs"][h], r["ag"][:, heads[h]], 0, 0).astype(BF16)
    first_stage((("v", 0), ("v", 1)), dot(r["normed_t"][...], r["dv"][...]))
    for h in range(2):
        k, v = r["qkv"][1, :, heads[h]], r["qkv"][2, :, heads[h]]
        for s in range(SLABS):
            at = pl.ds(s * PAD, PAD)
            dprobs = dot(r["ag"][at, heads[h]], v, 1, 1)
            probs = r["probs"][h, at, :].astype(F32)
            delta = jnp.sum(probs * dprobs, axis=-1, keepdims=True)
            ds = (probs * (dprobs - delta) * factor).astype(BF16)
            r["ds"][h, at, :] = ds
            r["dqk"][at, heads[0]] = dot(ds, k).astype(BF16)
        r["dqk"][:, heads[1]] = dot(r["ds"][h], r["qkv"][0, :, heads[h]], 0, 0).astype(BF16)
        first_stage((("q", h), ("k", h)), dot(r["normed_t"][...], r["dqk"][...]))

    wait_bytes(r["attin"], a_come)
    mixed = r["block_in"][...].astype(F32) + dot(r["att"][0], r["ow"][0], 1, 1)
    for s in (1, 2, 3):
        mixed = mixed + dot(r["attin"][s - 1], r["ow"][s], 1, 1)
    mixed = jnp.where(r["sc_col"][pl.ds(0, PAD), :] < 0.0, mixed, 0.0)
    r["done"][0] = mixed[:SLOT].astype(BF16)
    block_write = pltpu.make_async_copy(r["done"], r["block_out"], new_sem())
    block_write.start()

    for name, stage in FINISH:
        finish(name, stage)
    block_write.wait()
    for c in res_copies:
        c.wait_send()
    for c in u_cross:
        c.wait_send()
    wait_bytes(r["sbuf"].at[pl.ds(1, 2)], s_sent)
    wait_bytes(r["ubuf"].at[pl.ds(1, 2)], u_sent)
    wait_bytes(r["attin"], a_sent)
    for name in ORDER:
        wait_bytes(r["in", name], piece_sent[name])


def scratch():
    out = {
        "sems": pltpu.SemaphoreType.DMA((len(LOADED) + 2 + 6 + 18 + 2 + 33,)),
        "ow": pltpu.VMEM((SLABS, D, COLS), BF16),
        "wq": pltpu.VMEM((3, D, COLS), BF16),
        "res": pltpu.VMEM((4, 8, TOK_IN), F32),
        "sbuf": pltpu.VMEM((SLABS, PAD, D), BF16),
        "ubuf": pltpu.VMEM((SLABS, PAD, D), BF16),
        "sc_col": pltpu.VMEM((ROWS, 1), F32),
        "sc_row": pltpu.VMEM((8, ROWS), F32),
        "chan": pltpu.VMEM((ROWS, 32), BF16),
        "lev": pltpu.VMEM((ROWS, 7), BF16),
        "block_in": pltpu.VMEM((PAD, D), BF16),
        "normed": pltpu.VMEM((ROWS, D), BF16),
        "up": pltpu.VMEM((ROWS, D), BF16),
        "qkv": pltpu.VMEM((3, ROWS, COLS), BF16),
        "probs": pltpu.VMEM((2, ROWS, ROWS), BF16),
        "ds": pltpu.VMEM((2, ROWS, ROWS), BF16),
        "att": pltpu.VMEM((SLABS, PAD, COLS), BF16),
        "attin": pltpu.VMEM((SLABS - 1, PAD, COLS), BF16),
        "ag": pltpu.VMEM((ROWS, COLS), BF16),
        "dv": pltpu.VMEM((ROWS, COLS), BF16),
        "dqk": pltpu.VMEM((ROWS, COLS), BF16),
        "normed_t": pltpu.VMEM((D, ROWS), BF16),
        "l_stream": pltpu.VMEM((1, SLOT, D), BF16),
        "l_out_grad": pltpu.VMEM((1, SLOT, D), BF16),
        "done": pltpu.VMEM((1, SLOT, D), BF16),
        "l_residuals": pltpu.VMEM((1, 8, TOK_IN), F32),
        "l_token_slot": pltpu.VMEM((1, TOK_IMG), jnp.int32),
        "l_norm_gain": pltpu.VMEM((1, D), F32),
        "l_level_embed": pltpu.VMEM((NSCALE, D), BF16),
        "l_embed_weight": pltpu.VMEM((32, D), BF16),
        "l_teacher_map": pltpu.VMEM((TOK_IMG, TOK_IN), F32),
    }
    for name, order in ORDER.items():
        _, n2, n3 = (SIZE[a] for a in order)
        tail = (16, HEAD_DIM)
        out["gf", name] = pltpu.VMEM((64,) + tail, F32)
        out["gb", name] = pltpu.VMEM((64,) + tail, BF16)
        out["in", name] = pltpu.VMEM((63,) + tail, BF16)
        for stage, share in ((0, n2 * n3), (1, n3)):
            out["sf", stage, name] = pltpu.VMEM((share,) + tail, F32)
            out["sb", stage, name] = pltpu.VMEM((share,) + tail, BF16)
    return out


def hand_over(block_in, weight_in, block_out, qkv_out, out_out):
    block_out[...] = block_in[...]
    qkv_out[...] = weight_in[:3]
    out_out[...] = weight_in[3]


INPUTS = (
    "residuals",
    "stream",
    "token_slot",
    "level_embed",
    "embed_weight",
    "norm_gain",
    "qkv_weight",
    "out_weight",
    "out_grad",
    "teacher_map",
)
OUTPUTS = ("block_out", "weight_grad")


def per_device(*args):
    ins = dict(zip(INPUTS, args))
    ins["norm_gain"] = ins["norm_gain"].reshape(1, D)
    ins["teacher_map"] = jnp.asarray(teacher_matrix())
    buffers = scratch()
    vmem = pl.BlockSpec(memory_space=pltpu.VMEM)
    far = pl.BlockSpec(memory_space=pl.ANY)
    block_shape = jax.ShapeDtypeStruct((1, SLOT, D), BF16)
    block_out, weight_grad = pl.pallas_call(
        functools.partial(kernel, INPUTS + OUTPUTS + tuple(buffers)),
        out_shape=(block_shape, jax.ShapeDtypeStruct((4, 16, COLS), F32)),
        in_specs=[far] * len(INPUTS),
        out_specs=(far, vmem),
        scratch_shapes=list(buffers.values()),
        compiler_params=pltpu.CompilerParams(
            collective_id=0, has_side_effects=True, vmem_limit_bytes=56 << 20
        ),
    )(*[ins[n] for n in INPUTS])
    block_out, qkv_grad, out_grad = pl.pallas_call(
        hand_over,
        out_shape=(
            block_shape,
            jax.ShapeDtypeStruct((3, 16, COLS), F32),
            jax.ShapeDtypeStruct((16, COLS), F32),
        ),
        in_specs=[vmem] * 2,
        out_specs=(vmem,) * 3,
    )(block_out, weight_grad)
    return block_out, qkv_grad.transpose(1, 0, 2), out_grad


def solution(mesh):
    in_specs = (
        P("img", "tok", None),
        P("img", "tok", None),
        P("img", None),
        P(),
        P(),
        P(),
        P(),
        P(),
        P("img", "tok", None),
    )
    out_specs = (P("img", "tok", None), P("img", None, "tok"), P("img", "tok"))
    return jax.shard_map(
        per_device, mesh=mesh, in_specs=in_specs, out_specs=out_specs, check_vma=False
    )
```
